32 devices in a mesh: slab: 2 (over core), vel: 16 (over z, y, x).
Axes of the slice: x: 2, y: 2, z: 4, core: 2. Of those that a mesh axis runs over, the one named last changes fastest.
Arguments:
- f_start: float32 [4096, 2, 8, 128], P('vel', 'slab'), as said below
- links: int32 [3, 2, 8, 128], P(None, 'slab'), may hold values 0 or 1
- solid: int32 [2, 8, 128], P('slab'), may hold values 0 or 1
Outputs:
- f_final: float32 [4096, 2, 8, 128], P('vel', 'slab')
The draws below stay inside these ranges and needn't reach their ends.
Inputs may be any that keep to these rules, and one draw needn't show every extreme that they name: `f_start`: every entry is positive.
All inputs are finite; a program needn't handle non-finite values. No bound on the sum of `links` or of `solid` on one device may be relied on, other than what follows from the above.
Results may differ from the reference program's by a relative error of at most 0.0003.
Values sent between devices are 32-bit elements; how exact they have to be, the bound alone decides.
A program may use at most 64 MiB of HBM per device.

```python
import math
import jax
import jax.numpy as jnp
from jax import lax

NQ = 16
NY = 8
NZ = 128
STEPS = 2
SWEEPS = 2
NX = 2


def draw_f_start(key, part):
    keys = jax.random.split(jax.random.fold_in(key, 17), 4)
    total_vel = NQ ** 3
    grid = (NX, NY, NZ)
    matter_per_volume = jax.random.uniform(keys[0], grid, jnp.float32, 0.5, 2.0)
    factor = jax.random.uniform(keys[3], (total_vel,) + grid, jnp.float32, 0.5, 1.5)
    drift = jax.random.uniform(keys[1], (3,) + grid, jnp.float32, -0.5, 0.5)
    warmth = jax.random.uniform(keys[2], grid, jnp.float32, 0.6, 1.5)
    index = jnp.arange(total_vel).astype(jnp.int32)
    comps = jnp.stack([index % NQ, index // NQ % NQ, index // (NQ * NQ)]).astype(jnp.float32)
    lattice = (comps - (NQ - 1) / 2.0) * 0.6
    spread = jnp.zeros((total_vel,) + grid, jnp.float32)
    for axis_dim in range(3):
        offset = lattice[axis_dim][:, None, None, None] - drift[axis_dim][None]
        spread = spread + offset * offset
    return matter_per_volume * warmth ** (-1.5) * jnp.exp(-spread / (2.0 * warmth)) * factor


def place_ends(array, own_key, low, largest):
    shape = array.shape
    place = [jax.random.randint(jax.random.fold_in(own_key, axis), (), 0, shape[axis]) for axis in range(len(shape))]
    array = array.at[tuple(place)].set(low)
    longest = shape.index(max(shape))
    place[longest] = (place[longest] + 1) % shape[longest]
    return array.at[tuple(place)].set(largest)


def setup_inputs(seed: int = 0) -> dict:
    arg_keys = jax.random.split(jax.random.key(seed), 4)
    return {
        "f_start": draw_f_start(jax.random.fold_in(arg_keys[3], 71), 0),
        "links": place_ends((jax.random.randint(arg_keys[1], (3, NX, NY, NZ), 0, 4) < 3).astype(jnp.int32), jax.random.fold_in(arg_keys[1], 1), 0, 1),
        "solid": place_ends((jax.random.randint(arg_keys[2], (NX, NY, NZ), 0, 8) < 1).astype(jnp.int32), jax.random.fold_in(arg_keys[2], 1), 0, 1),
    }


SPACING = 0.6
COUPLING = 1.0
COURANT = 0.06
RELAXATION_FREQ = 0.5
VISCOUS_TO_HEAT = 2.0 / 3.0
QUAD_WEIGHT = SPACING ** 3 / (2.0 * math.pi) ** 1.5


def lattice_of(first, number):
    index = (first + jnp.arange(number)).astype(jnp.int32)
    comp_x = index % NQ
    comp_y = (index // NQ) % NQ
    comp_z = index // (NQ * NQ)
    stacked = jnp.stack([comp_x, comp_y, comp_z]).astype(jnp.float32)
    return (stacked - (NQ - 1) / 2.0) * SPACING


def moment_basis(lattice):
    overall_work_content = 0.5 * jnp.sum(lattice * lattice, axis=0)
    rows = [jnp.ones_like(overall_work_content), lattice[0], lattice[1], lattice[2], overall_work_content,
            lattice[0] * overall_work_content, lattice[1] * overall_work_content, lattice[2] * overall_work_content]
    return jnp.stack(rows) * QUAD_WEIGHT


def shift_down(values, axis_dim):
    pads = [(0, 0)] * values.ndim
    pads[axis_dim] = (1, 0)
    return lax.slice_in_dim(jnp.pad(values, pads), 0, values.shape[axis_dim], axis=axis_dim)


def shift_up(values, axis_dim):
    pads = [(0, 0)] * values.ndim
    pads[axis_dim] = (0, 1)
    return lax.slice_in_dim(jnp.pad(values, pads), 1, values.shape[axis_dim] + 1, axis=axis_dim)


def macro_state(predicted):
    matter_per_volume = predicted[0]
    mean_flow_vector = predicted[1:4] / matter_per_volume
    overall_work_content = predicted[4]
    fluid_hotness_level = (2.0 * overall_work_content / matter_per_volume - jnp.sum(mean_flow_vector * mean_flow_vector, axis=0)) / 3.0
    fluid_normal_stress = matter_per_volume * fluid_hotness_level
    heat_current_vector = predicted[5:8] - mean_flow_vector * (overall_work_content + fluid_normal_stress)
    relaxation_update = RELAXATION_FREQ * matter_per_volume * fluid_hotness_level ** 0.28
    profile_multiplier = (1.0 - VISCOUS_TO_HEAT) * heat_current_vector / (5.0 * fluid_normal_stress * fluid_hotness_level)
    perturbation_height = matter_per_volume * fluid_hotness_level ** -1.5
    return mean_flow_vector, fluid_hotness_level, relaxation_update, profile_multiplier, perturbation_height


def upwind_local(dist, speed, axis_dim):
    return jnp.where(speed > 0, shift_down(dist, axis_dim), shift_up(dist, axis_dim))


def transport(dist, upwind_x, lattice, particle_population, open_up, open_low, solid):
    mean_flow_vector, fluid_hotness_level, relaxation_update, profile_multiplier, perturbation_height = particle_population
    peculiar = lattice[:, :, None, None, None] - mean_flow_vector[:, None]
    acoustic_celerity_power = jnp.sum(peculiar * peculiar, axis=0)
    matching_arrangement = jnp.sum(peculiar * profile_multiplier[:, None], axis=0)
    relaxed_distribution_goal = perturbation_height * jnp.exp(-acoustic_celerity_power / (2.0 * fluid_hotness_level)) * (1.0 + matching_arrangement * (acoustic_celerity_power / fluid_hotness_level - 5.0))
    flux = jnp.zeros_like(dist)
    for axis_dim in range(3):
        speed = lattice[axis_dim][:, None, None, None]
        rising = speed > 0
        outward = jnp.where(rising, open_up[axis_dim], open_low[axis_dim])
        inward = jnp.where(rising, open_low[axis_dim], open_up[axis_dim])
        if axis_dim == 0:
            neighbour = upwind_x
        else:
            neighbour = upwind_local(dist, speed, axis_dim + 1)
        flux = flux + jnp.abs(speed) * (outward * dist - inward * neighbour)
    fresh = (dist - COURANT * flux + relaxation_update * relaxed_distribution_goal) / (1.0 + relaxation_update)
    return jnp.where(solid > 0, dist, fresh)


def reference(f_start, links, solid):
    total_vel = NQ ** 3
    open_up = links.astype(jnp.float32)
    open_low = jnp.stack([shift_down(open_up[0], 0), shift_down(open_up[1], 1), shift_down(open_up[2], 2)])
    count = jnp.sum(open_up, axis=0) + jnp.sum(open_low, axis=0)
    lattice = lattice_of(0, total_vel)
    basis = moment_basis(lattice)
    block_rows = 256
    blocks = total_vel // block_rows
    lattice_blocks = jnp.transpose(lattice.reshape(3, blocks, block_rows), (1, 0, 2))
    dist = f_start
    for repeat in range(STEPS):
        moments = jnp.dot(basis, dist.reshape(total_vel, -1), precision=lax.Precision.HIGHEST)
        moments = moments.reshape((8,) + dist.shape[1:])
        predicted = moments
        for sweeping in range(SWEEPS):
            beside_all = (shift_up(predicted, 1) * open_up[0] + shift_down(predicted, 1) * open_low[0]
                      + shift_up(predicted, 2) * open_up[1] + shift_down(predicted, 2) * open_low[1]
                      + shift_up(predicted, 3) * open_up[2] + shift_down(predicted, 3) * open_low[2])
            predicted = (moments + COUPLING * beside_all) / (1.0 + COUPLING * count)
        particle_population = macro_state(predicted)

        def advance(pair):
            piece, part_lattice = pair
            speed = part_lattice[0][:, None, None, None]
            upwind_x = upwind_local(piece, speed, 1)
            return transport(piece, upwind_x, part_lattice, particle_population, open_up, open_low, solid)

        stacked = dist.reshape((blocks, block_rows) + dist.shape[1:])
        dist = lax.map(advance, (stacked, lattice_blocks)).reshape(dist.shape)
    return dist
```

```python
import functools
import math

import jax
import jax.numpy as jnp
from jax import lax
from jax.experimental import pallas as pl
from jax.experimental.pallas import tpu as pltpu
from jax.sharding import PartitionSpec as P

NQ = 16
HALF = NQ // 2
SWEEPS = 2
MOMENTS = 8

SPACING = 0.6
COUPLING = 1.0
COURANT = 0.06
RELAXATION_FREQ = 0.5
VISCOUS_TO_HEAT = 2.0 / 3.0
QUAD_WEIGHT = SPACING**3 / (2.0 * math.pi) ** 1.5

MESH = pl.DeviceIdType.MESH


def speed_of(index):
    return (index.astype(jnp.float32) - (NQ - 1) / 2.0) * SPACING


def rolled(cells, shift, axis):
    size = cells.shape[axis]
    return pltpu.roll(cells, shift % size if isinstance(shift, int) else shift, axis)


def upper(cells):
    return jnp.concatenate([cells[1:], jnp.zeros_like(cells[:1])], axis=0)


def lower(cells):
    return jnp.concatenate([jnp.zeros_like(cells[:1]), cells[:-1]], axis=0)


def macro_state(predicted):
    rho = predicted[0]
    per_rho = 1.0 / rho
    u = [predicted[1 + a] * per_rho for a in range(3)]
    energy = predicted[4]
    temp = (2.0 * energy * per_rho - (u[0] * u[0] + u[1] * u[1] + u[2] * u[2])) / 3.0
    pressure = rho * temp
    nu = RELAXATION_FREQ * rho * jnp.exp(0.28 * jnp.log(temp))
    scale = (1.0 - VISCOUS_TO_HEAT) / (5.0 * pressure * temp)
    s = [(predicted[5 + a] - u[a] * (energy + pressure)) * scale for a in range(3)]
    root = lax.rsqrt(temp)
    return u, temp, nu, s, rho * (root * root * root)


def masked_state(predicted, solid):
    u, temp, nu, s, height = macro_state(predicted)
    fluid = solid == 0
    per_temp = jnp.where(fluid, 1.0 / temp, 1.0)
    u = [jnp.where(fluid, x, 0.0) for x in u]
    s = [jnp.where(fluid, x, 0.0) for x in s]
    inv = jnp.where(fluid, 1.0 / (1.0 + nu), 1.0)
    amp = jnp.where(fluid, height * (nu / (1.0 + nu)), 0.0)
    return u, per_temp, s, inv, amp


def goal_moments(u, per_temp, s, amp):
    def one(i, sums):
        xi = speed_of(i)
        new = []
        for a in range(3):
            c = xi - u[a]
            term = jnp.exp(-0.5 * (c * c * per_temp))
            row = [sums[a][0] + term]
            for k in range(1, 7):
                term = term * c
                row.append(sums[a][k] + term)
            new.append(tuple(row))
        return tuple(new)

    zero = jnp.zeros_like(per_temp)
    line = lax.fori_loop(0, NQ, one, tuple((zero,) * 7 for _ in range(3)), unroll=2)
    pairs, products, heats, lifts = {}, {}, {}, {}

    def add(m, a, n=1):
        return tuple(k + n * (a == d) for d, k in enumerate(m))

    def f(m):
        if m not in products:
            if m[:2] not in pairs:
                pairs[m[:2]] = line[0][m[0]] * line[1][m[1]]
            products[m] = pairs[m[:2]] * line[2][m[2]]
        return products[m]

    def q(m):
        if m not in heats:
            heats[m] = f(add(m, 0, 2)) + f(add(m, 1, 2)) + f(add(m, 2, 2))
        return heats[m]

    def lift(m):
        if m not in lifts:
            lifts[m] = per_temp * q(m) - 5.0 * f(m)
        return lifts[m]

    def total(m):
        out = f(m)
        for a in range(3):
            out = out + s[a] * lift(add(m, a))
        return out

    def total_q(m):
        out = q(m)
        for a in range(3):
            up = add(m, a)
            out = out + s[a] * (lift(add(up, 0, 2)) + lift(add(up, 1, 2)) + lift(add(up, 2, 2)))
        return out

    origin = (0, 0, 0)
    weight = amp * QUAD_WEIGHT
    p0 = total(origin) * weight
    p1 = [total(add(origin, a)) * weight for a in range(3)]
    p2 = {}
    for a in range(3):
        for b in range(a, 3):
            p2[a, b] = p2[b, a] = total(add(add(origin, a), b)) * weight
    p3 = [total_q(add(origin, a)) * weight for a in range(3)]
    half_uu = 0.5 * (u[0] * u[0] + u[1] * u[1] + u[2] * u[2])
    energy = (
        0.5 * (p2[0, 0] + p2[1, 1] + p2[2, 2])
        + (u[0] * p1[0] + u[1] * p1[1] + u[2] * p1[2])
        + half_uu * p0
    )
    out = [p0] + [p1[a] + u[a] * p0 for a in range(3)] + [energy]
    for a in range(3):
        out.append(
            0.5 * p3[a]
            + (u[0] * p2[a, 0] + u[1] * p2[a, 1] + u[2] * p2[a, 2])
            + half_uu * p1[a]
            + u[a] * energy
        )
    return out


def kernel(
    n_slab, n_vel, f_ref, links_ref, solid_ref, out_ref,
    f0, base, last, halo0, halo1, links_all, solid_all, send1, send2, gather_in, all1, all2,
    faces, coef, gx, pred,
    load_sem, link_sem, link_send, halo_recv, halo_send, rs_recv, rs_send, ag_recv, ag_send, out_sem,
):
    slab = lax.axis_index("slab")
    rank = lax.axis_index("vel")
    rows = f_ref.shape[0]
    first1 = n_vel // 2 - MOMENTS // 2
    first2 = n_vel // 2 + MOMENTS // 2
    plane1 = rank - first1
    plane2 = lax.rem(rank - first2 + n_vel, n_vel)
    reduces1 = (plane1 >= 0) & (plane1 < MOMENTS)
    reduces2 = plane2 < MOMENTS
    has_below = slab > 0
    has_above = slab < n_slab - 1

    def start_all(copies):
        for copy in copies:
            copy.start()

    loads = [
        pltpu.make_async_copy(f_ref, f0, load_sem.at[0]),
        pltpu.make_async_copy(links_ref, links_all.at[slab], load_sem.at[1]),
        pltpu.make_async_copy(solid_ref, solid_all.at[slab], load_sem.at[2]),
    ]
    start_all(loads)

    barrier = pltpu.get_barrier_semaphore()
    for step in range(n_slab):
        to_slab = lax.rem(slab + step, n_slab)

        def greet(i, _, to_slab=to_slab):
            pl.semaphore_signal(
                barrier, inc=1, device_id={"slab": to_slab, "vel": lax.rem(rank + i, n_vel)},
                device_id_type=MESH,
            )
            return 0

        lax.fori_loop(1 if step == 0 else 0, n_vel, greet, 0)

    def clear(low):
        def one(j, _):
            for i in range(HALF):
                zero = jnp.zeros(f0.shape[2:], jnp.float32)
                halo0[j, low + i] = zero
                halo1[j, low + i] = zero
            return 0

        lax.fori_loop(0, rows, one, 0)

    @pl.when(jnp.logical_not(has_below))
    def _():
        clear(HALF)

    @pl.when(jnp.logical_not(has_above))
    def _():
        clear(0)

    def row_speeds(j):
        row = rank * rows + j
        return lax.rem(row, NQ), lax.div(row, NQ)

    def add_row(sums, a0, a1, a2, a3, xi_y, xi_z):
        r = xi_y * xi_y + xi_z * xi_z
        e = 0.5 * (a2 + r * a0)
        return (
            sums[0] + a0, sums[1] + a1, sums[2] + xi_y * a0, sums[3] + xi_z * a0,
            sums[4] + e, sums[5] + 0.5 * (a3 + r * a1), sums[6] + xi_y * e, sums[7] + xi_z * e,
        )

    def moments_of(source):
        def one(j, sums):
            y, z = row_speeds(j)
            a0 = a1 = a2 = a3 = None
            for i in range(HALF):
                xi = (i + 0.5) * SPACING
                plus, minus = source[j, HALF + i], source[j, HALF - 1 - i]
                even, odd = plus + minus, plus - minus
                t = [even * QUAD_WEIGHT, odd * (QUAD_WEIGHT * xi),
                     even * (QUAD_WEIGHT * xi**2), odd * (QUAD_WEIGHT * xi**3)]
                if i == 0:
                    a0, a1, a2, a3 = t
                else:
                    a0, a1, a2, a3 = a0 + t[0], a1 + t[1], a2 + t[2], a3 + t[3]
            return add_row(sums, a0, a1, a2, a3, speed_of(y), speed_of(z))

        zero = jnp.zeros(f0.shape[2:], jnp.float32)
        return lax.fori_loop(0, rows, one, (zero,) * MOMENTS)

    loads[0].wait()
    m1 = moments_of(f0)
    for k in range(MOMENTS):
        send1[k] = m1[k]
    loads[1].wait()
    loads[2].wait()
    pl.semaphore_wait(barrier, n_slab * n_vel - 1)

    def scatter(source, first):
        def one(i, _):
            k = lax.rem(rank + i, MOMENTS)
            target = lax.rem(first + k, n_vel)

            @pl.when(target != rank)
            def _():
                pltpu.make_async_remote_copy(
                    src_ref=source.at[k], dst_ref=gather_in.at[rank],
                    send_sem=rs_send.at[0 if source is send1 else 1], recv_sem=rs_recv,
                    device_id={"vel": target}, device_id_type=MESH,
                ).start()

            return 0

        lax.fori_loop(0, MOMENTS, one, 0)

    scatter(send1, first1)

    for step in range(1, n_slab):
        to_slab = lax.rem(slab + step, n_slab)
        pltpu.make_async_remote_copy(
            src_ref=links_ref, dst_ref=links_all.at[slab], send_sem=link_send.at[0, step],
            recv_sem=link_sem.at[0], device_id={"slab": to_slab}, device_id_type=MESH,
        ).start()
        pltpu.make_async_remote_copy(
            src_ref=solid_ref, dst_ref=solid_all.at[slab], send_sem=link_send.at[1, step],
            recv_sem=link_sem.at[1], device_id={"slab": to_slab}, device_id_type=MESH,
        ).start()

    up_half, low_half = pl.ds(HALF, HALF), pl.ds(0, HALF)

    def halo_copy(source, halo, which, half):
        part = up_half if half else low_half
        to_slab = slab + 1 if half else slab - 1
        return pltpu.make_async_remote_copy(
            src_ref=source.at[:, part], dst_ref=halo.at[:, part],
            send_sem=halo_send.at[which, half], recv_sem=halo_recv.at[which, half],
            device_id={"slab": to_slab}, device_id_type=MESH,
        )

    def send_halo(source, halo, which):
        @pl.when(has_above)
        def _():
            halo_copy(source, halo, which, 1).start()

        @pl.when(has_below)
        def _():
            halo_copy(source, halo, which, 0).start()

    def wait_halo(source, halo, which, half):
        @pl.when(has_below if half else has_above)
        def _():
            halo_copy(source, halo, which, half).wait_recv()

    def wait_halo_send(source, halo, which):
        @pl.when(has_above)
        def _():
            halo_copy(source, halo, which, 1).wait_send()

        @pl.when(has_below)
        def _():
            halo_copy(source, halo, which, 0).wait_send()

    send_halo(f0, halo0, 0)

    if n_slab > 1:
        others = pl.ds(0, n_slab - 1)
        pltpu.make_async_copy(links_all.at[others], links_all.at[others], link_sem.at[0]).wait()
        pltpu.make_async_copy(solid_all.at[others], solid_all.at[others], link_sem.at[1]).wait()

    shape = (n_slab,) + f0.shape[2:]
    up = [links_all[:, a].astype(jnp.float32) for a in range(3)]
    at_y = lax.broadcasted_iota(jnp.int32, shape, 1)
    at_z = lax.broadcasted_iota(jnp.int32, shape, 2)
    at_x = lax.broadcasted_iota(jnp.int32, shape, 0)
    low = [
        lower(up[0]),
        jnp.where(at_y == 0, 0.0, rolled(up[1], 1, 1)),
        jnp.where(at_z == 0, 0.0, rolled(up[2], 1, 2)),
    ]
    up_in = [
        jnp.where(at_x == shape[0] - 1, 0.0, up[0]),
        jnp.where(at_y == shape[1] - 1, 0.0, up[1]),
        jnp.where(at_z == shape[2] - 1, 0.0, up[2]),
    ]
    count = up[0] + up[1] + up[2] + low[0] + low[1] + low[2]
    for a in range(3):
        faces[a] = up_in[a]
        faces[3 + a] = low[a]
    faces[6] = 1.0 / (1.0 + COUPLING * count)
    solid = solid_all[...]
    fluid = jnp.where(solid == 0, COURANT, 0.0)
    for a in range(3):
        pred[0] = fluid * low[a]
        pred[1] = fluid * up_in[a]
        pred[2] = fluid * up[a]
        coef[0, a, 0] = pred[0, slab]
        coef[0, a, 1] = pred[1, slab]
        coef[1, a, 0] = pred[2, slab]
        coef[1, a, 1] = pred[0, slab]

    def streamed(source, halo, half, first_row, row_end, finish):
        cells = f0.shape[2:]

        def one(j, carry):
            y, z = row_speeds(j)
            xi_y, xi_z = speed_of(y), speed_of(z)
            sign_y = jnp.where(y >= HALF, 1, 0)
            sign_z = jnp.where(z >= HALF, 1, 0)
            turn_y = jnp.where(y >= HALF, 1, cells[0] - 1)
            turn_z = jnp.where(z >= HALF, 1, cells[1] - 1)
            abs_y, abs_z = jnp.abs(xi_y), jnp.abs(xi_z)
            stay = 1.0 - (abs_y * coef[sign_y, 1, 0] + abs_z * coef[sign_z, 2, 0])
            in_y = abs_y * coef[sign_y, 1, 1]
            in_z = abs_z * coef[sign_z, 2, 1]
            out_x, in_x = coef[half, 0, 0], coef[half, 0, 1]
            extra = finish.row(j, xi_y, xi_z) if finish else None
            for i in range(HALF):
                ix = half * HALF + i
                abs_x = jnp.abs(speed_of(jnp.int32(ix))) if isinstance(ix, int) else jnp.abs(speed_of(ix))
                f = source[j, ix]
                value = (
                    f * (stay - abs_x * out_x)
                    + in_y * rolled(f, turn_y, 0)
                    + in_z * rolled(f, turn_z, 1)
                    + abs_x * (in_x * halo[j, ix])
                )
                if finish:
                    finish.store(j, ix, value, extra)
                else:
                    base[j, ix] = value
            return carry

        lax.fori_loop(first_row, row_end, one, 0)

    class Goal:
        def __init__(self, target, u, per_temp, s, inv, amp):
            self.target, self.u, self.per_temp, self.s, self.inv, self.amp = target, u, per_temp, s, inv, amp

            def one(i, _):
                c = speed_of(i) - u[0]
                part = c * c * per_temp
                gx[0, i] = jnp.exp(-0.5 * part)
                gx[1, i] = s[0] * c
                gx[2, i] = part
                return 0

            lax.fori_loop(0, NQ, one, 0, unroll=4)

        def row(self, j, xi_y, xi_z):
            c_y, c_z = xi_y - self.u[1], xi_z - self.u[2]
            part = (c_y * c_y + c_z * c_z) * self.per_temp
            return jnp.exp(-0.5 * part) * self.amp, self.s[1] * c_y + self.s[2] * c_z, part - 5.0

        def store(self, j, ix, value, extra):
            height, along, part = extra
            bell = gx[0, ix] * height
            self.target[j, ix] = value * self.inv + bell * (1.0 + (gx[1, ix] + along) * (gx[2, ix] + part))

    lead = jnp.where(has_above, 1, 0)

    def both_halves(body):
        for turn in range(2):
            body(lead if turn == 0 else 1 - lead, turn)

    def wait_dynamic(source, halo, which, half):
        @pl.when(half == 1)
        def _():
            wait_halo(source, halo, which, 1)

        @pl.when(half == 0)
        def _():
            wait_halo(source, halo, which, 0)

    def reduce_and_send(plane, source, everything, which):
        pltpu.make_async_copy(
            gather_in.at[pl.ds(0, n_vel - 1)], gather_in.at[pl.ds(0, n_vel - 1)], rs_recv
        ).wait()
        gather_in[rank] = source[plane]
        total = gather_in[0]
        for v in range(1, n_vel):
            total = total + gather_in[v]
        mine = plane * n_slab + slab
        everything[mine] = total
        for step in range(n_slab):
            to_slab = lax.rem(slab + step, n_slab)

            def one(i, _, to_slab=to_slab, step=step):
                pltpu.make_async_remote_copy(
                    src_ref=everything.at[mine], dst_ref=everything.at[mine],
                    send_sem=ag_send.at[step], recv_sem=ag_recv.at[which],
                    device_id={"slab": to_slab, "vel": lax.rem(rank + i, n_vel)}, device_id_type=MESH,
                ).start()
                return 0

            lax.fori_loop(1 if step == 0 else 0, n_vel, one, 0)

    def wait_gathered(everything, which, reduces):
        planes = MOMENTS * n_slab

        @pl.when(reduces)
        def _():
            part = everything.at[pl.ds(0, planes - 1)]
            pltpu.make_async_copy(part, part, ag_recv.at[which]).wait()

        @pl.when(jnp.logical_not(reduces))
        def _():
            pltpu.make_async_copy(everything, everything, ag_recv.at[which]).wait()

    def first_pass(half, turn):
        wait_dynamic(f0, halo0, 0, half)
        streamed(f0, halo0, half, 0, rows, None)

    first_pass(lead, 0)

    @pl.when(reduces1)
    def _():
        reduce_and_send(plane1, send1, all1, 0)

    first_pass(1 - lead, 1)
    m2 = moments_of(base)
    for k in range(MOMENTS):
        send2[k] = m2[k]
    scatter(send2, first2)

    def predict(moments):
        now = moments
        for _ in range(SWEEPS):
            beside = (
                upper(now) * faces[0] + lower(now) * faces[3]
                + rolled(now, -1, 1) * faces[1] + rolled(now, 1, 1) * faces[4]
                + rolled(now, -1, 2) * faces[2] + rolled(now, 1, 2) * faces[5]
            )
            now = (moments + COUPLING * beside) * faces[6]
        return now

    wait_gathered(all1, 0, reduces1)
    state1 = [predict(all1[k * n_slab:(k + 1) * n_slab]) for k in range(MOMENTS)]
    u, per_temp, s, inv, amp = masked_state(state1, solid)

    def own(planes):
        for k, plane in enumerate(planes):
            pred[k] = plane
        return [pred[k, slab] for k in range(len(planes))]

    near = own([*u, per_temp, *s, inv])
    near_amp = own([amp])[0]
    goal = Goal(base, near[0:3], near[3], near[4:7], near[7], near_amp)

    def relax_rows(half):
        def one(j, carry):
            y, z = row_speeds(j)
            extra = goal.row(j, speed_of(y), speed_of(z))
            for i in range(HALF):
                goal.store(j, half * HALF + i, base[j, half * HALF + i], extra)
            return carry

        lax.fori_loop(0, rows, one, 0)

    relax_rows(lead)

    @pl.when(lead == 1)
    def _():
        @pl.when(has_above)
        def _():
            halo_copy(base, halo1, 1, 1).start()

    @pl.when(lead == 0)
    def _():
        @pl.when(has_below)
        def _():
            halo_copy(base, halo1, 1, 0).start()

    @pl.when(reduces2)
    def _():
        reduce_and_send(plane2, send2, all2, 1)

    relax_rows(1 - lead)

    @pl.when(jnp.logical_and(lead == 1, has_below))
    def _():
        halo_copy(base, halo1, 1, 0).start()

    target = goal_moments(u, per_temp, s, amp)

    wait_gathered(all2, 1, reduces2)
    state2 = [
        predict(all2[k * n_slab:(k + 1) * n_slab] * inv + target[k]) for k in range(MOMENTS)
    ]
    u, per_temp, s, inv, amp = masked_state(state2, solid)
    near = own([*u, per_temp, *s, inv])
    near_amp = own([amp])[0]
    final = Goal(last, near[0:3], near[3], near[4:7], near[7], near_amp)

    stores = []

    def last_pass(half, turn):
        wait_dynamic(base, halo1, 1, half)
        cut = rows // 2
        for piece in range(2):
            streamed(base, halo1, half, piece * cut, (piece + 1) * cut, final)
            where = (pl.ds(piece * cut, cut), pl.ds(half * HALF, HALF))
            copy = pltpu.make_async_copy(last.at[where], out_ref.at[where], out_sem.at[turn, piece])
            copy.start()
            stores.append(copy)

    both_halves(last_pass)

    wait_halo_send(f0, halo0, 0)
    wait_halo_send(base, halo1, 1)
    for step in range(1, n_slab):
        pltpu.make_async_copy(links_all.at[0], links_all.at[0], link_send.at[0, step]).wait()
        pltpu.make_async_copy(solid_all.at[0], solid_all.at[0], link_send.at[1, step]).wait()
    for which, reduces in ((0, reduces1), (1, reduces2)):
        source = send1 if which == 0 else send2

        @pl.when(reduces)
        def _():
            part = source.at[pl.ds(0, MOMENTS - 1)]
            pltpu.make_async_copy(part, part, rs_send.at[which]).wait()
            for step in range(n_slab):
                part = gather_in.at[pl.ds(0, n_vel - 1 if step == 0 else n_vel)]
                pltpu.make_async_copy(part, part, ag_send.at[step]).wait()

        @pl.when(jnp.logical_not(reduces))
        def _():
            pltpu.make_async_copy(source, source, rs_send.at[which]).wait()

    for copy in stores:
        copy.wait()


def body(f_start, links, solid):
    n_slab, n_vel = lax.axis_size("slab"), lax.axis_size("vel")
    vel_local, planes = f_start.shape[:2]
    cells = f_start.shape[2:]
    rows = vel_local // NQ
    assert planes == 1 and rows * NQ == vel_local and rows % 2 == 0 and n_vel >= 2 * MOMENTS
    f32, vmem, dma = jnp.float32, pltpu.VMEM, pltpu.SemaphoreType.DMA
    block = (rows, NQ) + cells
    grid = (n_slab,) + cells
    any_spec = pl.BlockSpec(memory_space=pl.ANY)
    out = pl.pallas_call(
        functools.partial(kernel, n_slab, n_vel),
        out_shape=jax.ShapeDtypeStruct(block, f32),
        in_specs=[any_spec] * 3,
        out_specs=any_spec,
        scratch_shapes=[
            vmem(block, f32), vmem(block, f32), vmem(block, f32), vmem(block, f32), vmem(block, f32),
            vmem((n_slab, 3) + cells, jnp.int32), vmem(grid, jnp.int32),
            vmem((MOMENTS,) + cells, f32), vmem((MOMENTS,) + cells, f32),
            vmem((n_vel,) + cells, f32),
            vmem((MOMENTS * n_slab,) + cells, f32), vmem((MOMENTS * n_slab,) + cells, f32),
            vmem((7,) + grid, f32), vmem((2, 3, 2) + cells, f32), vmem((3, NQ) + cells, f32),
            vmem((MOMENTS,) + grid, f32),
            dma((3,)), dma((2,)), dma((2, n_slab)), dma((2, 2)), dma((2, 2)), dma, dma((2,)),
            dma((2,)), dma((n_slab,)), dma((2, 2)),
        ],
        compiler_params=pltpu.CompilerParams(
            collective_id=0, has_side_effects=True, vmem_limit_bytes=32 * 1024 * 1024
        ),
    )(f_start.reshape(block), links.reshape((3,) + cells), solid.reshape(cells))
    return out.reshape(f_start.shape)


def solution(mesh):
    in_specs = (P("vel", "slab", None, None), P(None, "slab", None, None), P("slab", None, None))
    out_specs = P("vel", "slab", None, None)
    return jax.shard_map(body, mesh=mesh, in_specs=in_specs, out_specs=out_specs, check_vma=False)
```

```python
import functools
import math

import jax
import jax.numpy as jnp
from jax import lax
from jax.experimental import pallas as pl
from jax.experimental.pallas import tpu as pltpu
from jax.sharding import PartitionSpec as P

NQ = 16
HALF = NQ // 2
SWEEPS = 2
MOMENTS = 8

SPACING = 0.6
COUPLING = 1.0
COURANT = 0.06
RELAXATION_FREQ = 0.5
VISCOUS_TO_HEAT = 2.0 / 3.0
QUAD_WEIGHT = SPACING**3 / (2.0 * math.pi) ** 1.5

MESH = pl.DeviceIdType.MESH


def speed_of(index):
    return (index.astype(jnp.float32) - (NQ - 1) / 2.0) * SPACING


def rolled(cells, shift, axis):
    size = cells.shape[axis]
    return pltpu.roll(cells, shift % size if isinstance(shift, int) else shift, axis)


def upper(cells):
    return jnp.concatenate([cells[1:], jnp.zeros_like(cells[:1])], axis=0)


def lower(cells):
    return jnp.concatenate([jnp.zeros_like(cells[:1]), cells[:-1]], axis=0)


def macro_state(predicted):
    rho = predicted[0]
    per_rho = 1.0 / rho
    u = [predicted[1 + a] * per_rho for a in range(3)]
    energy = predicted[4]
    temp = (2.0 * energy * per_rho - (u[0] * u[0] + u[1] * u[1] + u[2] * u[2])) / 3.0
    pressure = rho * temp
    nu = RELAXATION_FREQ * rho * jnp.exp(0.28 * jnp.log(temp))
    scale = (1.0 - VISCOUS_TO_HEAT) / (5.0 * pressure * temp)
    s = [(predicted[5 + a] - u[a] * (energy + pressure)) * scale for a in range(3)]
    root = lax.rsqrt(temp)
    return u, temp, nu, s, rho * (root * root * root)


def masked_state(predicted, solid):
    u, temp, nu, s, height = macro_state(predicted)
    fluid = solid == 0
    per_temp = jnp.where(fluid, 1.0 / temp, 1.0)
    u = [jnp.where(fluid, x, 0.0) for x in u]
    s = [jnp.where(fluid, x, 0.0) for x in s]
    inv = jnp.where(fluid, 1.0 / (1.0 + nu), 1.0)
    amp = jnp.where(fluid, height * (nu / (1.0 + nu)), 0.0)
    return u, per_temp, s, inv, amp


def goal_moments(u, per_temp, s, amp):
    def one(i, sums):
        xi = speed_of(i)
        new = []
        for a in range(3):
            c = xi - u[a]
            term = jnp.exp(-0.5 * (c * c * per_temp))
            row = [sums[a][0] + term]
            for k in range(1, 7):
                term = term * c
                row.append(sums[a][k] + term)
            new.append(tuple(row))
        return tuple(new)

    zero = jnp.zeros_like(per_temp)
    line = lax.fori_loop(0, NQ, one, tuple((zero,) * 7 for _ in range(3)), unroll=4)
    pairs, products, heats, lifts = {}, {}, {}, {}

    def add(m, a, n=1):
        return tuple(k + n * (a == d) for d, k in enumerate(m))

    def f(m):
        if m not in products:
            if m[:2] not in pairs:
                pairs[m[:2]] = line[0][m[0]] * line[1][m[1]]
            products[m] = pairs[m[:2]] * line[2][m[2]]
        return products[m]

    def q(m):
        if m not in heats:
            heats[m] = f(add(m, 0, 2)) + f(add(m, 1, 2)) + f(add(m, 2, 2))
        return heats[m]

    def lift(m):
        if m not in lifts:
            lifts[m] = per_temp * q(m) - 5.0 * f(m)
        return lifts[m]

    def total(m):
        out = f(m)
        for a in range(3):
            out = out + s[a] * lift(add(m, a))
        return out

    def total_q(m):
        out = q(m)
        for a in range(3):
            up = add(m, a)
            out = out + s[a] * (lift(add(up, 0, 2)) + lift(add(up, 1, 2)) + lift(add(up, 2, 2)))
        return out

    origin = (0, 0, 0)
    weight = amp * QUAD_WEIGHT
    p0 = total(origin) * weight
    p1 = [total(add(origin, a)) * weight for a in range(3)]
    p2 = {}
    for a in range(3):
        for b in range(a, 3):
            p2[a, b] = p2[b, a] = total(add(add(origin, a), b)) * weight
    p3 = [total_q(add(origin, a)) * weight for a in range(3)]
    half_uu = 0.5 * (u[0] * u[0] + u[1] * u[1] + u[2] * u[2])
    energy = (
        0.5 * (p2[0, 0] + p2[1, 1] + p2[2, 2])
        + (u[0] * p1[0] + u[1] * p1[1] + u[2] * p1[2])
        + half_uu * p0
    )
    out = [p0] + [p1[a] + u[a] * p0 for a in range(3)] + [energy]
    for a in range(3):
        out.append(
            0.5 * p3[a]
            + (u[0] * p2[a, 0] + u[1] * p2[a, 1] + u[2] * p2[a, 2])
            + half_uu * p1[a]
            + u[a] * energy
        )
    return out


def kernel(
    n_slab, n_vel, f_ref, links_ref, solid_ref, out_ref,
    f0, base, last, halo0, halo1, links_all, solid_all, send1, send2, gather_in, all1, all2,
    faces, coef, gx, pred,
    load_sem, link_sem, link_send, halo_recv, halo_send, rs_recv, rs_send, ag_recv, ag_send, out_sem,
):
    slab = lax.axis_index("slab")
    rank = lax.axis_index("vel")
    rows = f_ref.shape[0]
    first1 = n_vel // 2 - MOMENTS // 2
    first2 = n_vel // 2 + MOMENTS // 2
    plane1 = rank - first1
    plane2 = lax.rem(rank - first2 + n_vel, n_vel)
    reduces1 = (plane1 >= 0) & (plane1 < MOMENTS)
    reduces2 = plane2 < MOMENTS
    has_below = slab > 0
    has_above = slab < n_slab - 1

    def start_all(copies):
        for copy in copies:
            copy.start()

    loads = [
        pltpu.make_async_copy(f_ref, f0, load_sem.at[0]),
        pltpu.make_async_copy(links_ref, links_all.at[slab], load_sem.at[1]),
        pltpu.make_async_copy(solid_ref, solid_all.at[slab], load_sem.at[2]),
    ]
    start_all(loads)

    barrier = pltpu.get_barrier_semaphore()
    for step in range(n_slab):
        to_slab = lax.rem(slab + step, n_slab)

        def greet(i, _, to_slab=to_slab):
            pl.semaphore_signal(
                barrier, inc=1, device_id={"slab": to_slab, "vel": lax.rem(rank + i, n_vel)},
                device_id_type=MESH,
            )
            return 0

        lax.fori_loop(1 if step == 0 else 0, n_vel, greet, 0, unroll=5 if step == 0 else 4)

    def clear(low):
        def one(j, _):
            for i in range(HALF):
                zero = jnp.zeros(f0.shape[2:], jnp.float32)
                halo0[j, low + i] = zero
                halo1[j, low + i] = zero
            return 0

        lax.fori_loop(0, rows, one, 0)

    @pl.when(jnp.logical_not(has_below))
    def _():
        clear(HALF)

    @pl.when(jnp.logical_not(has_above))
    def _():
        clear(0)

    def row_speeds(j):
        row = rank * rows + j
        return lax.rem(row, NQ), lax.div(row, NQ)

    def add_row(sums, a0, a1, a2, a3, xi_y, xi_z):
        r = xi_y * xi_y + xi_z * xi_z
        e = 0.5 * (a2 + r * a0)
        return (
            sums[0] + a0, sums[1] + a1, sums[2] + xi_y * a0, sums[3] + xi_z * a0,
            sums[4] + e, sums[5] + 0.5 * (a3 + r * a1), sums[6] + xi_y * e, sums[7] + xi_z * e,
        )

    def moments_of(source):
        def one(j, sums):
            y, z = row_speeds(j)
            a0 = a1 = a2 = a3 = None
            for i in range(HALF):
                xi = (i + 0.5) * SPACING
                plus, minus = source[j, HALF + i], source[j, HALF - 1 - i]
                even, odd = plus + minus, plus - minus
                t = [even * QUAD_WEIGHT, odd * (QUAD_WEIGHT * xi),
                     even * (QUAD_WEIGHT * xi**2), odd * (QUAD_WEIGHT * xi**3)]
                if i == 0:
                    a0, a1, a2, a3 = t
                else:
                    a0, a1, a2, a3 = a0 + t[0], a1 + t[1], a2 + t[2], a3 + t[3]
            return add_row(sums, a0, a1, a2, a3, speed_of(y), speed_of(z))

        zero = jnp.zeros(f0.shape[2:], jnp.float32)
        return lax.fori_loop(0, rows, one, (zero,) * MOMENTS, unroll=2)

    loads[0].wait()
    m1 = moments_of(f0)
    for k in range(MOMENTS):
        send1[k] = m1[k]
    loads[1].wait()
    loads[2].wait()
    pl.semaphore_wait(barrier, n_slab * n_vel - 1)

    def scatter(source, first):
        def one(i, _):
            k = lax.rem(rank + i, MOMENTS)
            target = lax.rem(first + k, n_vel)

            @pl.when(target != rank)
            def _():
                pltpu.make_async_remote_copy(
                    src_ref=source.at[k], dst_ref=gather_in.at[rank],
                    send_sem=rs_send.at[0 if source is send1 else 1], recv_sem=rs_recv,
                    device_id={"vel": target}, device_id_type=MESH,
                ).start()

            return 0

        lax.fori_loop(0, MOMENTS, one, 0, unroll=True)

    scatter(send1, first1)

    for step in range(1, n_slab):
        to_slab = lax.rem(slab + step, n_slab)
        pltpu.make_async_remote_copy(
            src_ref=links_ref, dst_ref=links_all.at[slab], send_sem=link_send.at[0, step],
            recv_sem=link_sem.at[0], device_id={"slab": to_slab}, device_id_type=MESH,
        ).start()
        pltpu.make_async_remote_copy(
            src_ref=solid_ref, dst_ref=solid_all.at[slab], send_sem=link_send.at[1, step],
            recv_sem=link_sem.at[1], device_id={"slab": to_slab}, device_id_type=MESH,
        ).start()

    up_half, low_half = pl.ds(HALF, HALF), pl.ds(0, HALF)

    def halo_copy(source, halo, which, half):
        part = up_half if half else low_half
        to_slab = slab + 1 if half else slab - 1
        return pltpu.make_async_remote_copy(
            src_ref=source.at[:, part], dst_ref=halo.at[:, part],
            send_sem=halo_send.at[which, half], recv_sem=halo_recv.at[which, half],
            device_id={"slab": to_slab}, device_id_type=MESH,
        )

    def send_halo(source, halo, which):
        @pl.when(has_above)
        def _():
            halo_copy(source, halo, which, 1).start()

        @pl.when(has_below)
        def _():
            halo_copy(source, halo, which, 0).start()

    def wait_halo(source, halo, which, half):
        @pl.when(has_below if half else has_above)
        def _():
            halo_copy(source, halo, which, half).wait_recv()

    def wait_halo_send(source, halo, which):
        @pl.when(has_above)
        def _():
            halo_copy(source, halo, which, 1).wait_send()

        @pl.when(has_below)
        def _():
            halo_copy(source, halo, which, 0).wait_send()

    send_halo(f0, halo0, 0)

    if n_slab > 1:
        others = pl.ds(0, n_slab - 1)
        pltpu.make_async_copy(links_all.at[others], links_all.at[others], link_sem.at[0]).wait()
        pltpu.make_async_copy(solid_all.at[others], solid_all.at[others], link_sem.at[1]).wait()

    shape = (n_slab,) + f0.shape[2:]
    up = [links_all[:, a].astype(jnp.float32) for a in range(3)]
    at_y = lax.broadcasted_iota(jnp.int32, shape, 1)
    at_z = lax.broadcasted_iota(jnp.int32, shape, 2)
    at_x = lax.broadcasted_iota(jnp.int32, shape, 0)
    low = [
        lower(up[0]),
        jnp.where(at_y == 0, 0.0, rolled(up[1], 1, 1)),
        jnp.where(at_z == 0, 0.0, rolled(up[2], 1, 2)),
    ]
    up_in = [
        jnp.where(at_x == shape[0] - 1, 0.0, up[0]),
        jnp.where(at_y == shape[1] - 1, 0.0, up[1]),
        jnp.where(at_z == shape[2] - 1, 0.0, up[2]),
    ]
    count = up[0] + up[1] + up[2] + low[0] + low[1] + low[2]
    for a in range(3):
        faces[a] = up_in[a]
        faces[3 + a] = low[a]
    faces[6] = 1.0 / (1.0 + COUPLING * count)
    solid = solid_all[...]
    fluid = jnp.where(solid == 0, COURANT, 0.0)
    for a in range(3):
        pred[0] = fluid * low[a]
        pred[1] = fluid * up_in[a]
        pred[2] = fluid * up[a]
        coef[0, a, 0] = pred[0, slab]
        coef[0, a, 1] = pred[1, slab]
        coef[1, a, 0] = pred[2, slab]
        coef[1, a, 1] = pred[0, slab]

    def streamed(source, halo, half, first_row, row_end, finish):
        cells = f0.shape[2:]
        abs_of = [jnp.abs(speed_of(half * HALF + i)) for i in range(HALF)]

        def one(j, carry):
            y, z = row_speeds(j)
            xi_y, xi_z = speed_of(y), speed_of(z)
            sign_y = jnp.where(y >= HALF, 1, 0)
            sign_z = jnp.where(z >= HALF, 1, 0)
            turn_y = jnp.where(y >= HALF, 1, cells[0] - 1)
            turn_z = jnp.where(z >= HALF, 1, cells[1] - 1)
            abs_y, abs_z = jnp.abs(xi_y), jnp.abs(xi_z)
            stay = 1.0 - (abs_y * coef[sign_y, 1, 0] + abs_z * coef[sign_z, 2, 0])
            in_y = abs_y * coef[sign_y, 1, 1]
            in_z = abs_z * coef[sign_z, 2, 1]
            out_x, in_x = coef[half, 0, 0], coef[half, 0, 1]
            extra = finish.row(j, xi_y, xi_z) if finish else None
            for i in range(HALF):
                ix = half * HALF + i
                abs_x = abs_of[i]
                f = source[j, ix]
                value = (
                    f * (stay - abs_x * out_x)
                    + in_y * rolled(f, turn_y, 0)
                    + in_z * rolled(f, turn_z, 1)
                    + abs_x * (in_x * halo[j, ix])
                )
                if finish:
                    finish.store(j, ix, value, extra)
                else:
                    base[j, ix] = value
            return carry

        lax.fori_loop(first_row, row_end, one, 0, unroll=math.gcd(4, row_end - first_row))

    class Goal:
        def __init__(self, target, u, per_temp, s, inv, amp):
            self.target, self.u, self.per_temp, self.s, self.inv, self.amp = target, u, per_temp, s, inv, amp

            def one(i, _):
                c = speed_of(i) - u[0]
                part = c * c * per_temp
                gx[0, i] = jnp.exp(-0.5 * part)
                gx[1, i] = s[0] * c
                gx[2, i] = part
                return 0

            lax.fori_loop(0, NQ, one, 0, unroll=4)

        def row(self, j, xi_y, xi_z):
            c_y, c_z = xi_y - self.u[1], xi_z - self.u[2]
            part = (c_y * c_y + c_z * c_z) * self.per_temp
            return jnp.exp(-0.5 * part) * self.amp, self.s[1] * c_y + self.s[2] * c_z, part - 5.0

        def store(self, j, ix, value, extra):
            height, along, part = extra
            bell = gx[0, ix] * height
            self.target[j, ix] = value * self.inv + bell * (1.0 + (gx[1, ix] + along) * (gx[2, ix] + part))

    lead = jnp.where(has_above, 1, 0)

    def both_halves(body):
        for turn in range(2):
            body(lead if turn == 0 else 1 - lead, turn)

    def wait_dynamic(source, halo, which, half):
        @pl.when(half == 1)
        def _():
            wait_halo(source, halo, which, 1)

        @pl.when(half == 0)
        def _():
            wait_halo(source, halo, which, 0)

    def reduce_and_send(plane, source, everything, which):
        pltpu.make_async_copy(
            gather_in.at[pl.ds(0, n_vel - 1)], gather_in.at[pl.ds(0, n_vel - 1)], rs_recv
        ).wait()
        gather_in[rank] = source[plane]
        total = gather_in[0]
        for v in range(1, n_vel):
            total = total + gather_in[v]
        mine = plane * n_slab + slab
        everything[mine] = total
        for step in range(n_slab):
            to_slab = lax.rem(slab + step, n_slab)

            def one(i, _, to_slab=to_slab, step=step):
                pltpu.make_async_remote_copy(
                    src_ref=everything.at[mine], dst_ref=everything.at[mine],
                    send_sem=ag_send.at[step], recv_sem=ag_recv.at[which],
                    device_id={"slab": to_slab, "vel": lax.rem(rank + i, n_vel)}, device_id_type=MESH,
                ).start()
                return 0

            lax.fori_loop(1 if step == 0 else 0, n_vel, one, 0, unroll=5 if step == 0 else 4)

    def wait_gathered(everything, which, reduces):
        planes = MOMENTS * n_slab

        @pl.when(reduces)
        def _():
            part = everything.at[pl.ds(0, planes - 1)]
            pltpu.make_async_copy(part, part, ag_recv.at[which]).wait()

        @pl.when(jnp.logical_not(reduces))
        def _():
            pltpu.make_async_copy(everything, everything, ag_recv.at[which]).wait()

    def first_pass(half, turn):
        wait_dynamic(f0, halo0, 0, half)
        streamed(f0, halo0, half, 0, rows, None)

    first_pass(lead, 0)

    @pl.when(reduces1)
    def _():
        reduce_and_send(plane1, send1, all1, 0)

    first_pass(1 - lead, 1)
    m2 = moments_of(base)
    for k in range(MOMENTS):
        send2[k] = m2[k]
    scatter(send2, first2)

    def predict(moments):
        now = moments
        for _ in range(SWEEPS):
            beside = (
                upper(now) * faces[0] + lower(now) * faces[3]
                + rolled(now, -1, 1) * faces[1] + rolled(now, 1, 1) * faces[4]
                + rolled(now, -1, 2) * faces[2] + rolled(now, 1, 2) * faces[5]
            )
            now = (moments + COUPLING * beside) * faces[6]
        return now

    wait_gathered(all1, 0, reduces1)
    state1 = [predict(all1[k * n_slab:(k + 1) * n_slab]) for k in range(MOMENTS)]
    u, per_temp, s, inv, amp = masked_state(state1, solid)

    def own(planes):
        for k, plane in enumerate(planes):
            pred[k] = plane
        return [pred[k, slab] for k in range(len(planes))]

    near = own([*u, per_temp, *s, inv])
    near_amp = own([amp])[0]
    goal = Goal(base, near[0:3], near[3], near[4:7], near[7], near_amp)

    def relax_rows(half):
        def one(j, carry):
            y, z = row_speeds(j)
            extra = goal.row(j, speed_of(y), speed_of(z))
            for i in range(HALF):
                goal.store(j, half * HALF + i, base[j, half * HALF + i], extra)
            return carry

        lax.fori_loop(0, rows, one, 0, unroll=math.gcd(4, rows))

    relax_rows(lead)

    @pl.when(lead == 1)
    def _():
        @pl.when(has_above)
        def _():
            halo_copy(base, halo1, 1, 1).start()

    @pl.when(lead == 0)
    def _():
        @pl.when(has_below)
        def _():
            halo_copy(base, halo1, 1, 0).start()

    @pl.when(reduces2)
    def _():
        reduce_and_send(plane2, send2, all2, 1)

    relax_rows(1 - lead)

    @pl.when(jnp.logical_and(lead == 1, has_below))
    def _():
        halo_copy(base, halo1, 1, 0).start()

    target = goal_moments(u, per_temp, s, amp)

    wait_gathered(all2, 1, reduces2)
    state2 = [
        predict(all2[k * n_slab:(k + 1) * n_slab] * inv + target[k]) for k in range(MOMENTS)
    ]
    u, per_temp, s, inv, amp = masked_state(state2, solid)
    near = own([*u, per_temp, *s, inv])
    near_amp = own([amp])[0]
    final = Goal(last, near[0:3], near[3], near[4:7], near[7], near_amp)

    stores = []

    def last_pass(half, turn):
        wait_dynamic(base, halo1, 1, half)
        cut = rows // 2
        for piece in range(2):
            streamed(base, halo1, half, piece * cut, (piece + 1) * cut, final)
            where = (pl.ds(piece * cut, cut), pl.ds(half * HALF, HALF))
            copy = pltpu.make_async_copy(last.at[where], out_ref.at[where], out_sem.at[turn, piece])
            copy.start()
            stores.append(copy)

    both_halves(last_pass)

    wait_halo_send(f0, halo0, 0)
    wait_halo_send(base, halo1, 1)
    for step in range(1, n_slab):
        pltpu.make_async_copy(links_all.at[0], links_all.at[0], link_send.at[0, step]).wait()
        pltpu.make_async_copy(solid_all.at[0], solid_all.at[0], link_send.at[1, step]).wait()
    for which, reduces in ((0, reduces1), (1, reduces2)):
        source = send1 if which == 0 else send2

        @pl.when(reduces)
        def _():
            part = source.at[pl.ds(0, MOMENTS - 1)]
            pltpu.make_async_copy(part, part, rs_send.at[which]).wait()
            for step in range(n_slab):
                part = gather_in.at[pl.ds(0, n_vel - 1 if step == 0 else n_vel)]
                pltpu.make_async_copy(part, part, ag_send.at[step]).wait()

        @pl.when(jnp.logical_not(reduces))
        def _():
            pltpu.make_async_copy(source, source, rs_send.at[which]).wait()

    for copy in stores:
        copy.wait()


def body(f_start, links, solid):
    n_slab, n_vel = lax.axis_size("slab"), lax.axis_size("vel")
    vel_local, planes = f_start.shape[:2]
    cells = f_start.shape[2:]
    rows = vel_local // NQ
    assert planes == 1 and rows * NQ == vel_local and rows % 2 == 0 and n_vel >= 2 * MOMENTS
    f32, vmem, dma = jnp.float32, pltpu.VMEM, pltpu.SemaphoreType.DMA
    block = (rows, NQ) + cells
    grid = (n_slab,) + cells
    any_spec = pl.BlockSpec(memory_space=pltpu.HBM)
    out = pl.pallas_call(
        functools.partial(kernel, n_slab, n_vel),
        out_shape=jax.ShapeDtypeStruct(block, f32),
        in_specs=[any_spec] * 3,
        out_specs=any_spec,
        scratch_shapes=[
            vmem(block, f32), vmem(block, f32), vmem(block, f32), vmem(block, f32), vmem(block, f32),
            vmem((n_slab, 3) + cells, jnp.int32), vmem(grid, jnp.int32),
            vmem((MOMENTS,) + cells, f32), vmem((MOMENTS,) + cells, f32),
            vmem((n_vel,) + cells, f32),
            vmem((MOMENTS * n_slab,) + cells, f32), vmem((MOMENTS * n_slab,) + cells, f32),
            vmem((7,) + grid, f32), vmem((2, 3, 2) + cells, f32), vmem((3, NQ) + cells, f32),
            vmem((MOMENTS,) + grid, f32),
            dma((3,)), dma((2,)), dma((2, n_slab)), dma((2, 2)), dma((2, 2)), dma, dma((2,)),
            dma((2,)), dma((n_slab,)), dma((2, 2)),
        ],
        compiler_params=pltpu.CompilerParams(
            collective_id=0, has_side_effects=True, vmem_limit_bytes=32 * 1024 * 1024
        ),
    )(f_start.reshape(block), links.reshape((3,) + cells), solid.reshape(cells))
    return out.reshape(f_start.shape)


def solution(mesh):
    in_specs = (P("vel", "slab", None, None), P(None, "slab", None, None), P("slab", None, None))
    out_specs = P("vel", "slab", None, None)
    return jax.shard_map(body, mesh=mesh, in_specs=in_specs, out_specs=out_specs, check_vma=False)
```

```python
import functools
import math

import jax
import jax.numpy as jnp
from jax import lax
from jax.experimental import pallas as pl
from jax.experimental.pallas import tpu as pltpu
from jax.sharding import PartitionSpec as P

NQ = 16
HALF = NQ // 2
SWEEPS = 2
MOMENTS = 8

SPACING = 0.6
COUPLING = 1.0
COURANT = 0.06
RELAXATION_FREQ = 0.5
VISCOUS_TO_HEAT = 2.0 / 3.0
QUAD_WEIGHT = SPACING**3 / (2.0 * math.pi) ** 1.5

MESH = pl.DeviceIdType.MESH


def speed_of(index):
    return (index.astype(jnp.float32) - (NQ - 1) / 2.0) * SPACING


def rolled(cells, shift, axis):
    size = cells.shape[axis]
    return pltpu.roll(cells, shift % size if isinstance(shift, int) else shift, axis)


def upper(cells):
    return jnp.concatenate([cells[1:], jnp.zeros_like(cells[:1])], axis=0)


def lower(cells):
    return jnp.concatenate([jnp.zeros_like(cells[:1]), cells[:-1]], axis=0)


def macro_state(predicted):
    rho = predicted[0]
    per_rho = 1.0 / rho
    u = [predicted[1 + a] * per_rho for a in range(3)]
    energy = predicted[4]
    temp = (2.0 * energy * per_rho - (u[0] * u[0] + u[1] * u[1] + u[2] * u[2])) / 3.0
    pressure = rho * temp
    nu = RELAXATION_FREQ * rho * jnp.exp(0.28 * jnp.log(temp))
    scale = (1.0 - VISCOUS_TO_HEAT) / (5.0 * pressure * temp)
    s = [(predicted[5 + a] - u[a] * (energy + pressure)) * scale for a in range(3)]
    root = lax.rsqrt(temp)
    return u, temp, nu, s, rho * (root * root * root)


def masked_state(predicted, solid):
    u, temp, nu, s, height = macro_state(predicted)
    fluid = solid == 0
    per_temp = jnp.where(fluid, 1.0 / temp, 1.0)
    u = [jnp.where(fluid, x, 0.0) for x in u]
    s = [jnp.where(fluid, x, 0.0) for x in s]
    inv = jnp.where(fluid, 1.0 / (1.0 + nu), 1.0)
    amp = jnp.where(fluid, height * (nu / (1.0 + nu)), 0.0)
    return u, per_temp, s, inv, amp


def goal_moments(u, per_temp, s, amp):
    def one(i, sums):
        xi = speed_of(i)
        new = []
        for a in range(3):
            c = xi - u[a]
            term = jnp.exp(-0.5 * (c * c * per_temp))
            row = [sums[a][0] + term]
            for k in range(1, 7):
                term = term * c
                row.append(sums[a][k] + term)
            new.append(tuple(row))
        return tuple(new)

    zero = jnp.zeros_like(per_temp)
    line = lax.fori_loop(0, NQ, one, tuple((zero,) * 7 for _ in range(3)), unroll=4)
    pairs, products, heats, lifts = {}, {}, {}, {}

    def add(m, a, n=1):
        return tuple(k + n * (a == d) for d, k in enumerate(m))

    def f(m):
        if m not in products:
            if m[:2] not in pairs:
                pairs[m[:2]] = line[0][m[0]] * line[1][m[1]]
            products[m] = pairs[m[:2]] * line[2][m[2]]
        return products[m]

    def q(m):
        if m not in heats:
            heats[m] = f(add(m, 0, 2)) + f(add(m, 1, 2)) + f(add(m, 2, 2))
        return heats[m]

    def lift(m):
        if m not in lifts:
            lifts[m] = per_temp * q(m) - 5.0 * f(m)
        return lifts[m]

    def total(m):
        out = f(m)
        for a in range(3):
            out = out + s[a] * lift(add(m, a))
        return out

    def total_q(m):
        out = q(m)
        for a in range(3):
            up = add(m, a)
            out = out + s[a] * (lift(add(up, 0, 2)) + lift(add(up, 1, 2)) + lift(add(up, 2, 2)))
        return out

    origin = (0, 0, 0)
    weight = amp * QUAD_WEIGHT
    p0 = total(origin) * weight
    p1 = [total(add(origin, a)) * weight for a in range(3)]
    p2 = {}
    for a in range(3):
        for b in range(a, 3):
            p2[a, b] = p2[b, a] = total(add(add(origin, a), b)) * weight
    p3 = [total_q(add(origin, a)) * weight for a in range(3)]
    half_uu = 0.5 * (u[0] * u[0] + u[1] * u[1] + u[2] * u[2])
    energy = (
        0.5 * (p2[0, 0] + p2[1, 1] + p2[2, 2])
        + (u[0] * p1[0] + u[1] * p1[1] + u[2] * p1[2])
        + half_uu * p0
    )
    out = [p0] + [p1[a] + u[a] * p0 for a in range(3)] + [energy]
    for a in range(3):
        out.append(
            0.5 * p3[a]
            + (u[0] * p2[a, 0] + u[1] * p2[a, 1] + u[2] * p2[a, 2])
            + half_uu * p1[a]
            + u[a] * energy
        )
    return out


def kernel(
    n_slab, n_vel, f_ref, links_ref, solid_ref, out_ref,
    f0, base, last, halo0, halo1, links_all, solid_all, send1, send2, gather_in, all1, all2,
    faces, coef, gx, pred,
    load_sem, link_sem, link_send, halo_recv, halo_send, rs_recv, rs_send, ag_recv, ag_send, out_sem,
):
    slab = lax.axis_index("slab")
    rank = lax.axis_index("vel")
    rows = f_ref.shape[0]
    first1 = n_vel // 2 - MOMENTS // 2
    first2 = n_vel // 2 + MOMENTS // 2
    plane1 = rank - first1
    plane2 = lax.rem(rank - first2 + n_vel, n_vel)
    reduces1 = (plane1 >= 0) & (plane1 < MOMENTS)
    reduces2 = plane2 < MOMENTS
    has_below = slab > 0
    has_above = slab < n_slab - 1

    def start_all(copies):
        for copy in copies:
            copy.start()

    loads = [
        pltpu.make_async_copy(f_ref, f0, load_sem.at[0]),
        pltpu.make_async_copy(links_ref, links_all.at[slab], load_sem.at[1]),
        pltpu.make_async_copy(solid_ref, solid_all.at[slab], load_sem.at[2]),
    ]
    start_all(loads)

    barrier = pltpu.get_barrier_semaphore()
    for step in range(n_slab):
        to_slab = lax.rem(slab + step, n_slab)

        def greet(i, _, to_slab=to_slab):
            pl.semaphore_signal(
                barrier, inc=1, device_id={"slab": to_slab, "vel": lax.rem(rank + i, n_vel)},
                device_id_type=MESH,
            )
            return 0

        lax.fori_loop(1 if step == 0 else 0, n_vel, greet, 0, unroll=5 if step == 0 else 4)

    def clear(low):
        def one(j, _):
            for i in range(HALF):
                zero = jnp.zeros(f0.shape[2:], jnp.float32)
                halo0[j, low + i] = zero
                halo1[j, low + i] = zero
            return 0

        lax.fori_loop(0, rows, one, 0)

    @pl.when(jnp.logical_not(has_below))
    def _():
        clear(HALF)

    @pl.when(jnp.logical_not(has_above))
    def _():
        clear(0)

    def row_speeds(j):
        row = rank * rows + j
        return lax.rem(row, NQ), lax.div(row, NQ)

    def add_row(sums, a0, a1, a2, a3, xi_y, xi_z):
        r = xi_y * xi_y + xi_z * xi_z
        e = 0.5 * (a2 + r * a0)
        return (
            sums[0] + a0, sums[1] + a1, sums[2] + xi_y * a0, sums[3] + xi_z * a0,
            sums[4] + e, sums[5] + 0.5 * (a3 + r * a1), sums[6] + xi_y * e, sums[7] + xi_z * e,
        )

    def moments_of(source):
        def one(j, sums):
            y, z = row_speeds(j)
            a0 = a1 = a2 = a3 = None
            for i in range(HALF):
                xi = (i + 0.5) * SPACING
                plus, minus = source[j, HALF + i], source[j, HALF - 1 - i]
                even, odd = plus + minus, plus - minus
                t = [even * QUAD_WEIGHT, odd * (QUAD_WEIGHT * xi),
                     even * (QUAD_WEIGHT * xi**2), odd * (QUAD_WEIGHT * xi**3)]
                if i == 0:
                    a0, a1, a2, a3 = t
                else:
                    a0, a1, a2, a3 = a0 + t[0], a1 + t[1], a2 + t[2], a3 + t[3]
            return add_row(sums, a0, a1, a2, a3, speed_of(y), speed_of(z))

        zero = jnp.zeros(f0.shape[2:], jnp.float32)
        return lax.fori_loop(0, rows, one, (zero,) * MOMENTS, unroll=2)

    loads[0].wait()
    m1 = moments_of(f0)
    for k in range(MOMENTS):
        send1[k] = m1[k]
    loads[1].wait()
    loads[2].wait()
    pl.semaphore_wait(barrier, n_slab * n_vel - 1)

    def scatter(source, first):
        def one(i, _):
            k = lax.rem(rank + i, MOMENTS)
            target = lax.rem(first + k, n_vel)

            @pl.when(target != rank)
            def _():
                pltpu.make_async_remote_copy(
                    src_ref=source.at[k], dst_ref=gather_in.at[rank],
                    send_sem=rs_send.at[0 if source is send1 else 1], recv_sem=rs_recv,
                    device_id={"vel": target}, device_id_type=MESH,
                ).start()

            return 0

        lax.fori_loop(0, MOMENTS, one, 0, unroll=True)

    scatter(send1, first1)

    for step in range(1, n_slab):
        to_slab = lax.rem(slab + step, n_slab)
        pltpu.make_async_remote_copy(
            src_ref=links_ref, dst_ref=links_all.at[slab], send_sem=link_send.at[0, step],
            recv_sem=link_sem.at[0], device_id={"slab": to_slab}, device_id_type=MESH,
        ).start()
        pltpu.make_async_remote_copy(
            src_ref=solid_ref, dst_ref=solid_all.at[slab], send_sem=link_send.at[1, step],
            recv_sem=link_sem.at[1], device_id={"slab": to_slab}, device_id_type=MESH,
        ).start()

    up_half, low_half = pl.ds(HALF, HALF), pl.ds(0, HALF)

    def halo_copy(source, halo, which, half):
        part = up_half if half else low_half
        to_slab = slab + 1 if half else slab - 1
        return pltpu.make_async_remote_copy(
            src_ref=source.at[:, part], dst_ref=halo.at[:, part],
            send_sem=halo_send.at[which, half], recv_sem=halo_recv.at[which, half],
            device_id={"slab": to_slab}, device_id_type=MESH,
        )

    def send_halo(source, halo, which):
        @pl.when(has_above)
        def _():
            halo_copy(source, halo, which, 1).start()

        @pl.when(has_below)
        def _():
            halo_copy(source, halo, which, 0).start()

    def wait_halo(source, halo, which, half):
        @pl.when(has_below if half else has_above)
        def _():
            halo_copy(source, halo, which, half).wait_recv()

    def wait_halo_send(source, halo, which):
        @pl.when(has_above)
        def _():
            halo_copy(source, halo, which, 1).wait_send()

        @pl.when(has_below)
        def _():
            halo_copy(source, halo, which, 0).wait_send()

    send_halo(f0, halo0, 0)

    if n_slab > 1:
        others = pl.ds(0, n_slab - 1)
        pltpu.make_async_copy(links_all.at[others], links_all.at[others], link_sem.at[0]).wait()
        pltpu.make_async_copy(solid_all.at[others], solid_all.at[others], link_sem.at[1]).wait()

    shape = (n_slab,) + f0.shape[2:]
    up = [links_all[:, a].astype(jnp.float32) for a in range(3)]
    at_y = lax.broadcasted_iota(jnp.int32, shape, 1)
    at_z = lax.broadcasted_iota(jnp.int32, shape, 2)
    at_x = lax.broadcasted_iota(jnp.int32, shape, 0)
    low = [
        lower(up[0]),
        jnp.where(at_y == 0, 0.0, rolled(up[1], 1, 1)),
        jnp.where(at_z == 0, 0.0, rolled(up[2], 1, 2)),
    ]
    up_in = [
        jnp.where(at_x == shape[0] - 1, 0.0, up[0]),
        jnp.where(at_y == shape[1] - 1, 0.0, up[1]),
        jnp.where(at_z == shape[2] - 1, 0.0, up[2]),
    ]
    count = up[0] + up[1] + up[2] + low[0] + low[1] + low[2]
    for a in range(3):
        faces[a] = up_in[a]
        faces[3 + a] = low[a]
    faces[6] = 1.0 / (1.0 + COUPLING * count)
    solid = solid_all[...]
    fluid = jnp.where(solid == 0, COURANT, 0.0)
    for a in range(3):
        pred[0] = fluid * low[a]
        pred[1] = fluid * up_in[a]
        pred[2] = fluid * up[a]
        coef[0, a, 0] = pred[0, slab]
        coef[0, a, 1] = pred[1, slab]
        coef[1, a, 0] = pred[2, slab]
        coef[1, a, 1] = pred[0, slab]

    def streamed(source, halo, half, first_row, row_end, finish):
        cells = f0.shape[2:]
        abs_of = [jnp.abs(speed_of(half * HALF + i)) for i in range(HALF)]

        def one(j, carry):
            y, z = row_speeds(j)
            xi_y, xi_z = speed_of(y), speed_of(z)
            sign_y = jnp.where(y >= HALF, 1, 0)
            sign_z = jnp.where(z >= HALF, 1, 0)
            turn_y = jnp.where(y >= HALF, 1, cells[0] - 1)
            turn_z = jnp.where(z >= HALF, 1, cells[1] - 1)
            abs_y, abs_z = jnp.abs(xi_y), jnp.abs(xi_z)
            stay = 1.0 - (abs_y * coef[sign_y, 1, 0] + abs_z * coef[sign_z, 2, 0])
            in_y = abs_y * coef[sign_y, 1, 1]
            in_z = abs_z * coef[sign_z, 2, 1]
            out_x, in_x = coef[half, 0, 0], coef[half, 0, 1]
            extra = finish.row(j, xi_y, xi_z) if finish else None
            for i in range(HALF):
                ix = half * HALF + i
                abs_x = abs_of[i]
                f = source[j, ix]
                value = (
                    f * (stay - abs_x * out_x)
                    + in_y * rolled(f, turn_y, 0)
                    + in_z * rolled(f, turn_z, 1)
                    + abs_x * (in_x * halo[j, ix])
                )
                if finish:
                    finish.store(j, ix, value, extra)
                else:
                    base[j, ix] = value
            return carry

        lax.fori_loop(first_row, row_end, one, 0, unroll=math.gcd(4, row_end - first_row))

    class Goal:
        def __init__(self, target, u, per_temp, s, inv, amp):
            self.target, self.u, self.per_temp, self.s, self.inv, self.amp = target, u, per_temp, s, inv, amp

            def one(i, _):
                c = speed_of(i) - u[0]
                part = c * c * per_temp
                gx[0, i] = jnp.exp(-0.5 * part)
                gx[1, i] = s[0] * c
                gx[2, i] = part
                return 0

            lax.fori_loop(0, NQ, one, 0, unroll=4)

        def row(self, j, xi_y, xi_z):
            c_y, c_z = xi_y - self.u[1], xi_z - self.u[2]
            part = (c_y * c_y + c_z * c_z) * self.per_temp
            return jnp.exp(-0.5 * part) * self.amp, self.s[1] * c_y + self.s[2] * c_z, part - 5.0

        def store(self, j, ix, value, extra):
            height, along, part = extra
            bell = gx[0, ix] * height
            self.target[j, ix] = value * self.inv + bell * (1.0 + (gx[1, ix] + along) * (gx[2, ix] + part))

    lead = jnp.where(has_above, 1, 0)

    def both_halves(body):
        for turn in range(2):
            body(lead if turn == 0 else 1 - lead, turn)

    def wait_dynamic(source, halo, which, half):
        @pl.when(half == 1)
        def _():
            wait_halo(source, halo, which, 1)

        @pl.when(half == 0)
        def _():
            wait_halo(source, halo, which, 0)

    def reduce_and_send(plane, source, everything, which):
        pltpu.make_async_copy(
            gather_in.at[pl.ds(0, n_vel - 1)], gather_in.at[pl.ds(0, n_vel - 1)], rs_recv
        ).wait()
        gather_in[rank] = source[plane]
        total = gather_in[0]
        for v in range(1, n_vel):
            total = total + gather_in[v]
        mine = plane * n_slab + slab
        everything[mine] = total
        for step in range(n_slab):
            to_slab = lax.rem(slab + step, n_slab)

            def one(i, _, to_slab=to_slab, step=step):
                pltpu.make_async_remote_copy(
                    src_ref=everything.at[mine], dst_ref=everything.at[mine],
                    send_sem=ag_send.at[step], recv_sem=ag_recv.at[which],
                    device_id={"slab": to_slab, "vel": lax.rem(rank + i, n_vel)}, device_id_type=MESH,
                ).start()
                return 0

            lax.fori_loop(1 if step == 0 else 0, n_vel, one, 0, unroll=5 if step == 0 else 4)

    def wait_gathered(everything, which, reduces):
        planes = MOMENTS * n_slab

        @pl.when(reduces)
        def _():
            part = everything.at[pl.ds(0, planes - 1)]
            pltpu.make_async_copy(part, part, ag_recv.at[which]).wait()

        @pl.when(jnp.logical_not(reduces))
        def _():
            pltpu.make_async_copy(everything, everything, ag_recv.at[which]).wait()

    def first_pass(half, turn):
        wait_dynamic(f0, halo0, 0, half)
        streamed(f0, halo0, half, 0, rows, None)

    first_pass(lead, 0)

    first_pass(1 - lead, 1)
    m2 = moments_of(base)
    for k in range(MOMENTS):
        send2[k] = m2[k]
    scatter(send2, first2)

    @pl.when(reduces1)
    def _():
        reduce_and_send(plane1, send1, all1, 0)

    def predict(moments):
        now = moments
        for _ in range(SWEEPS):
            beside = (
                upper(now) * faces[0] + lower(now) * faces[3]
                + rolled(now, -1, 1) * faces[1] + rolled(now, 1, 1) * faces[4]
                + rolled(now, -1, 2) * faces[2] + rolled(now, 1, 2) * faces[5]
            )
            now = (moments + COUPLING * beside) * faces[6]
        return now

    @pl.when(reduces2)
    def _():
        reduce_and_send(plane2, send2, all2, 1)

    wait_gathered(all1, 0, reduces1)
    state1 = [predict(all1[k * n_slab:(k + 1) * n_slab]) for k in range(MOMENTS)]
    u, per_temp, s, inv, amp = masked_state(state1, solid)

    def own(planes):
        for k, plane in enumerate(planes):
            pred[k] = plane
        return [pred[k, slab] for k in range(len(planes))]

    near = own([*u, per_temp, *s, inv])
    near_amp = own([amp])[0]
    goal = Goal(base, near[0:3], near[3], near[4:7], near[7], near_amp)

    def relax_rows(half):
        def one(j, carry):
            y, z = row_speeds(j)
            extra = goal.row(j, speed_of(y), speed_of(z))
            for i in range(HALF):
                goal.store(j, half * HALF + i, base[j, half * HALF + i], extra)
            return carry

        lax.fori_loop(0, rows, one, 0, unroll=math.gcd(4, rows))

    relax_rows(lead)

    @pl.when(lead == 1)
    def _():
        @pl.when(has_above)
        def _():
            halo_copy(base, halo1, 1, 1).start()

    @pl.when(lead == 0)
    def _():
        @pl.when(has_below)
        def _():
            halo_copy(base, halo1, 1, 0).start()

    relax_rows(1 - lead)

    @pl.when(jnp.logical_and(lead == 1, has_below))
    def _():
        halo_copy(base, halo1, 1, 0).start()

    target = goal_moments(u, per_temp, s, amp)

    wait_gathered(all2, 1, reduces2)
    state2 = [
        predict(all2[k * n_slab:(k + 1) * n_slab] * inv + target[k]) for k in range(MOMENTS)
    ]
    u, per_temp, s, inv, amp = masked_state(state2, solid)
    near = own([*u, per_temp, *s, inv])
    near_amp = own([amp])[0]
    final = Goal(last, near[0:3], near[3], near[4:7], near[7], near_amp)

    stores = []

    def last_pass(half, turn):
        wait_dynamic(base, halo1, 1, half)
        cut = rows // 2
        for piece in range(2):
            streamed(base, halo1, half, piece * cut, (piece + 1) * cut, final)
            where = (pl.ds(piece * cut, cut), pl.ds(half * HALF, HALF))
            copy = pltpu.make_async_copy(last.at[where], out_ref.at[where], out_sem.at[turn, piece])
            copy.start()
            stores.append(copy)

    both_halves(last_pass)

    wait_halo_send(f0, halo0, 0)
    wait_halo_send(base, halo1, 1)
    for step in range(1, n_slab):
        pltpu.make_async_copy(links_all.at[0], links_all.at[0], link_send.at[0, step]).wait()
        pltpu.make_async_copy(solid_all.at[0], solid_all.at[0], link_send.at[1, step]).wait()
    for which, reduces in ((0, reduces1), (1, reduces2)):
        source = send1 if which == 0 else send2

        @pl.when(reduces)
        def _():
            part = source.at[pl.ds(0, MOMENTS - 1)]
            pltpu.make_async_copy(part, part, rs_send.at[which]).wait()
            for step in range(n_slab):
                part = gather_in.at[pl.ds(0, n_vel - 1 if step == 0 else n_vel)]
                pltpu.make_async_copy(part, part, ag_send.at[step]).wait()

        @pl.when(jnp.logical_not(reduces))
        def _():
            pltpu.make_async_copy(source, source, rs_send.at[which]).wait()

    for copy in stores:
        copy.wait()


def body(f_start, links, solid):
    n_slab, n_vel = lax.axis_size("slab"), lax.axis_size("vel")
    vel_local, planes = f_start.shape[:2]
    cells = f_start.shape[2:]
    rows = vel_local // NQ
    assert planes == 1 and rows * NQ == vel_local and rows % 2 == 0 and n_vel >= 2 * MOMENTS
    f32, vmem, dma = jnp.float32, pltpu.VMEM, pltpu.SemaphoreType.DMA
    block = (rows, NQ) + cells
    grid = (n_slab,) + cells
    any_spec = pl.BlockSpec(memory_space=pltpu.HBM)
    out = pl.pallas_call(
        functools.partial(kernel, n_slab, n_vel),
        out_shape=jax.ShapeDtypeStruct(block, f32),
        in_specs=[any_spec] * 3,
        out_specs=any_spec,
        scratch_shapes=[
            vmem(block, f32), vmem(block, f32), vmem(block, f32), vmem(block, f32), vmem(block, f32),
            vmem((n_slab, 3) + cells, jnp.int32), vmem(grid, jnp.int32),
            vmem((MOMENTS,) + cells, f32), vmem((MOMENTS,) + cells, f32),
            vmem((n_vel,) + cells, f32),
            vmem((MOMENTS * n_slab,) + cells, f32), vmem((MOMENTS * n_slab,) + cells, f32),
            vmem((7,) + grid, f32), vmem((2, 3, 2) + cells, f32), vmem((3, NQ) + cells, f32),
            vmem((MOMENTS,) + grid, f32),
            dma((3,)), dma((2,)), dma((2, n_slab)), dma((2, 2)), dma((2, 2)), dma, dma((2,)),
            dma((2,)), dma((n_slab,)), dma((2, 2)),
        ],
        compiler_params=pltpu.CompilerParams(
            collective_id=0, has_side_effects=True, vmem_limit_bytes=60 * 1024 * 1024
        ),
    )(f_start.reshape(block), links.reshape((3,) + cells), solid.reshape(cells))
    return out.reshape(f_start.shape)


def solution(mesh):
    in_specs = (P("vel", "slab", None, None), P(None, "slab", None, None), P("slab", None, None))
    out_specs = P("vel", "slab", None, None)
    return jax.shard_map(body, mesh=mesh, in_specs=in_specs, out_specs=out_specs, check_vma=False)
```

```python
import functools
import math

import jax
import jax.numpy as jnp
from jax import lax
from jax.experimental import pallas as pl
from jax.experimental.pallas import tpu as pltpu
from jax.sharding import PartitionSpec as P

NQ = 16
HALF = NQ // 2
SWEEPS = 2
MOMENTS = 8

SPACING = 0.6
COUPLING = 1.0
COURANT = 0.06
RELAXATION_FREQ = 0.5
VISCOUS_TO_HEAT = 2.0 / 3.0
QUAD_WEIGHT = SPACING**3 / (2.0 * math.pi) ** 1.5

MESH = pl.DeviceIdType.MESH


def speed_of(index):
    return (index.astype(jnp.float32) - (NQ - 1) / 2.0) * SPACING


def rolled(cells, shift, axis):
    size = cells.shape[axis]
    return pltpu.roll(cells, shift % size if isinstance(shift, int) else shift, axis)


def upper(cells):
    return jnp.concatenate([cells[1:], jnp.zeros_like(cells[:1])], axis=0)


def lower(cells):
    return jnp.concatenate([jnp.zeros_like(cells[:1]), cells[:-1]], axis=0)


def macro_state(predicted):
    rho = predicted[0]
    per_rho = 1.0 / rho
    u = [predicted[1 + a] * per_rho for a in range(3)]
    energy = predicted[4]
    temp = (2.0 * energy * per_rho - (u[0] * u[0] + u[1] * u[1] + u[2] * u[2])) / 3.0
    pressure = rho * temp
    nu = RELAXATION_FREQ * rho * jnp.exp(0.28 * jnp.log(temp))
    scale = (1.0 - VISCOUS_TO_HEAT) / (5.0 * pressure * temp)
    s = [(predicted[5 + a] - u[a] * (energy + pressure)) * scale for a in range(3)]
    root = lax.rsqrt(temp)
    return u, temp, nu, s, rho * (root * root * root)


def masked_state(predicted, solid):
    u, temp, nu, s, height = macro_state(predicted)
    fluid = solid == 0
    per_temp = jnp.where(fluid, 1.0 / temp, 1.0)
    u = [jnp.where(fluid, x, 0.0) for x in u]
    s = [jnp.where(fluid, x, 0.0) for x in s]
    inv = jnp.where(fluid, 1.0 / (1.0 + nu), 1.0)
    amp = jnp.where(fluid, height * (nu / (1.0 + nu)), 0.0)
    return u, per_temp, s, inv, amp


def goal_moments(u, per_temp, s, amp):
    def one(i, sums):
        xi = speed_of(i)
        new = []
        for a in range(3):
            c = xi - u[a]
            term = jnp.exp(-0.5 * (c * c * per_temp))
            row = [sums[a][0] + term]
            for k in range(1, 7):
                term = term * c
                row.append(sums[a][k] + term)
            new.append(tuple(row))
        return tuple(new)

    zero = jnp.zeros_like(per_temp)
    line = lax.fori_loop(0, NQ, one, tuple((zero,) * 7 for _ in range(3)), unroll=4)
    pairs, products, heats, lifts = {}, {}, {}, {}

    def add(m, a, n=1):
        return tuple(k + n * (a == d) for d, k in enumerate(m))

    def f(m):
        if m not in products:
            if m[:2] not in pairs:
                pairs[m[:2]] = line[0][m[0]] * line[1][m[1]]
            products[m] = pairs[m[:2]] * line[2][m[2]]
        return products[m]

    def q(m):
        if m not in heats:
            heats[m] = f(add(m, 0, 2)) + f(add(m, 1, 2)) + f(add(m, 2, 2))
        return heats[m]

    def lift(m):
        if m not in lifts:
            lifts[m] = per_temp * q(m) - 5.0 * f(m)
        return lifts[m]

    def total(m):
        out = f(m)
        for a in range(3):
            out = out + s[a] * lift(add(m, a))
        return out

    def total_q(m):
        out = q(m)
        for a in range(3):
            up = add(m, a)
            out = out + s[a] * (lift(add(up, 0, 2)) + lift(add(up, 1, 2)) + lift(add(up, 2, 2)))
        return out

    origin = (0, 0, 0)
    weight = amp * QUAD_WEIGHT
    p0 = total(origin) * weight
    p1 = [total(add(origin, a)) * weight for a in range(3)]
    p2 = {}
    for a in range(3):
        for b in range(a, 3):
            p2[a, b] = p2[b, a] = total(add(add(origin, a), b)) * weight
    p3 = [total_q(add(origin, a)) * weight for a in range(3)]
    half_uu = 0.5 * (u[0] * u[0] + u[1] * u[1] + u[2] * u[2])
    energy = (
        0.5 * (p2[0, 0] + p2[1, 1] + p2[2, 2])
        + (u[0] * p1[0] + u[1] * p1[1] + u[2] * p1[2])
        + half_uu * p0
    )
    out = [p0] + [p1[a] + u[a] * p0 for a in range(3)] + [energy]
    for a in range(3):
        out.append(
            0.5 * p3[a]
            + (u[0] * p2[a, 0] + u[1] * p2[a, 1] + u[2] * p2[a, 2])
            + half_uu * p1[a]
            + u[a] * energy
        )
    return out


def upwind(source, halo, coef, half, speeds, size, store, row=None):
    cells = source.shape[2:]
    abs_of = [jnp.abs(speed_of(jnp.asarray(half * HALF + i))) for i in range(HALF)]

    def one(j, carry):
        y, z = speeds(j)
        xi_y, xi_z = speed_of(y), speed_of(z)
        sign_y = jnp.where(y >= HALF, 1, 0)
        sign_z = jnp.where(z >= HALF, 1, 0)
        turn_y = jnp.where(y >= HALF, 1, cells[0] - 1)
        turn_z = jnp.where(z >= HALF, 1, cells[1] - 1)
        abs_y, abs_z = jnp.abs(xi_y), jnp.abs(xi_z)
        stay = 1.0 - (abs_y * coef[sign_y, 1, 0] + abs_z * coef[sign_z, 2, 0])
        in_y = abs_y * coef[sign_y, 1, 1]
        in_z = abs_z * coef[sign_z, 2, 1]
        out_x, in_x = coef[half, 0, 0], coef[half, 0, 1]
        extra = row(xi_y, xi_z) if row else None
        for i in range(HALF):
            ix = half * HALF + i
            f = source[j, ix]
            value = (
                f * (stay - abs_of[i] * out_x)
                + in_y * rolled(f, turn_y, 0)
                + in_z * rolled(f, turn_z, 1)
                + abs_of[i] * (in_x * halo[j, ix])
            )
            store(j, ix, value, extra)
        return carry

    lax.fori_loop(0, size, one, 0, unroll=math.gcd(4, size))


def fill_bells(gx, near):
    u, per_temp, s = near[0], near[3], near[4]

    def one(i, _):
        c = speed_of(i) - u
        part = c * c * per_temp
        gx[0, i] = jnp.exp(-0.5 * part)
        gx[1, i] = s * c
        gx[2, i] = part
        return 0

    lax.fori_loop(0, NQ, one, 0, unroll=4)


def bell_row(near, xi_y, xi_z):
    c_y, c_z = xi_y - near[1], xi_z - near[2]
    part = (c_y * c_y + c_z * c_z) * near[3]
    return jnp.exp(-0.5 * part) * near[8], near[5] * c_y + near[6] * c_z, part - 5.0


def relaxed(gx, near, ix, value, extra):
    height, along, part = extra
    return value * near[7] + gx[0, ix] * height * (1.0 + (gx[1, ix] + along) * (gx[2, ix] + part))


def last_kernel(rows, base_ref, halo_ref, state_ref, coef_ref, out_ref, gx):
    rank, piece = lax.axis_index("vel"), pl.program_id(0)
    size = base_ref.shape[0]
    near = [state_ref[k] for k in range(9)]

    @pl.when(piece == 0)
    def _():
        fill_bells(gx, near)

    def speeds(j):
        row = rank * rows + piece * size + j
        return lax.rem(row, NQ), lax.div(row, NQ)

    def store(j, ix, value, extra):
        out_ref[j, ix] = relaxed(gx, near, ix, value, extra)

    for half in range(2):
        upwind(base_ref, halo_ref, coef_ref, half, speeds, size, store, functools.partial(bell_row, near))


def kernel(
    n_slab, n_vel, f_ref, links_ref, solid_ref, base_out, halo1, state_out, coef_out,
    f0, base, halo0, state, links_all, solid_all, send1, send2, gather_in, all1, all2,
    faces, coef, gx, pred,
    load_sem, link_sem, link_send, halo_recv, halo_send, rs_recv, rs_send, ag_recv, ag_send, out_sem, zero_sem,
):
    slab = lax.axis_index("slab")
    rank = lax.axis_index("vel")
    rows = f_ref.shape[0]
    first1 = n_vel // 2 - MOMENTS // 2
    first2 = n_vel // 2 + MOMENTS // 2
    plane1 = rank - first1
    plane2 = lax.rem(rank - first2 + n_vel, n_vel)
    reduces1 = (plane1 >= 0) & (plane1 < MOMENTS)
    reduces2 = plane2 < MOMENTS
    has_below = slab > 0
    has_above = slab < n_slab - 1

    def start_all(copies):
        for copy in copies:
            copy.start()

    loads = [
        pltpu.make_async_copy(f_ref, f0, load_sem.at[0]),
        pltpu.make_async_copy(links_ref, links_all.at[slab], load_sem.at[1]),
        pltpu.make_async_copy(solid_ref, solid_all.at[slab], load_sem.at[2]),
    ]
    start_all(loads)

    barrier = pltpu.get_barrier_semaphore()
    for step in range(n_slab):
        to_slab = lax.rem(slab + step, n_slab)

        def greet(i, _, to_slab=to_slab):
            pl.semaphore_signal(
                barrier, inc=1, device_id={"slab": to_slab, "vel": lax.rem(rank + i, n_vel)},
                device_id_type=MESH,
            )
            return 0

        lax.fori_loop(1 if step == 0 else 0, n_vel, greet, 0, unroll=5 if step == 0 else 4)

    def clear(low):
        def one(j, _):
            for i in range(HALF):
                zero = jnp.zeros(f0.shape[2:], jnp.float32)
                halo0[j, low + i] = zero
            return 0

        lax.fori_loop(0, rows, one, 0)
        zero_copy(low).start()

    def zero_copy(low):
        where = (slice(None), pl.ds(low, HALF))
        return pltpu.make_async_copy(halo0.at[where], halo1.at[where], zero_sem.at[low // HALF])

    @pl.when(jnp.logical_not(has_below))
    def _():
        clear(HALF)

    @pl.when(jnp.logical_not(has_above))
    def _():
        clear(0)

    def row_speeds(j):
        row = rank * rows + j
        return lax.rem(row, NQ), lax.div(row, NQ)

    def add_row(sums, a0, a1, a2, a3, xi_y, xi_z):
        r = xi_y * xi_y + xi_z * xi_z
        e = 0.5 * (a2 + r * a0)
        return (
            sums[0] + a0, sums[1] + a1, sums[2] + xi_y * a0, sums[3] + xi_z * a0,
            sums[4] + e, sums[5] + 0.5 * (a3 + r * a1), sums[6] + xi_y * e, sums[7] + xi_z * e,
        )

    def moments_of(source):
        def one(j, sums):
            y, z = row_speeds(j)
            a0 = a1 = a2 = a3 = None
            for i in range(HALF):
                xi = (i + 0.5) * SPACING
                plus, minus = source[j, HALF + i], source[j, HALF - 1 - i]
                even, odd = plus + minus, plus - minus
                t = [even * QUAD_WEIGHT, odd * (QUAD_WEIGHT * xi),
                     even * (QUAD_WEIGHT * xi**2), odd * (QUAD_WEIGHT * xi**3)]
                if i == 0:
                    a0, a1, a2, a3 = t
                else:
                    a0, a1, a2, a3 = a0 + t[0], a1 + t[1], a2 + t[2], a3 + t[3]
            return add_row(sums, a0, a1, a2, a3, speed_of(y), speed_of(z))

        zero = jnp.zeros(f0.shape[2:], jnp.float32)
        return lax.fori_loop(0, rows, one, (zero,) * MOMENTS, unroll=2)

    loads[0].wait()
    m1 = moments_of(f0)
    for k in range(MOMENTS):
        send1[k] = m1[k]
    loads[1].wait()
    loads[2].wait()
    pl.semaphore_wait(barrier, n_slab * n_vel - 1)

    def scatter(source, first):
        def one(i, _):
            k = lax.rem(rank + i, MOMENTS)
            target = lax.rem(first + k, n_vel)

            @pl.when(target != rank)
            def _():
                pltpu.make_async_remote_copy(
                    src_ref=source.at[k], dst_ref=gather_in.at[rank],
                    send_sem=rs_send.at[0 if source is send1 else 1], recv_sem=rs_recv,
                    device_id={"vel": target}, device_id_type=MESH,
                ).start()

            return 0

        lax.fori_loop(0, MOMENTS, one, 0, unroll=True)

    scatter(send1, first1)

    for step in range(1, n_slab):
        to_slab = lax.rem(slab + step, n_slab)
        pltpu.make_async_remote_copy(
            src_ref=links_ref, dst_ref=links_all.at[slab], send_sem=link_send.at[0, step],
            recv_sem=link_sem.at[0], device_id={"slab": to_slab}, device_id_type=MESH,
        ).start()
        pltpu.make_async_remote_copy(
            src_ref=solid_ref, dst_ref=solid_all.at[slab], send_sem=link_send.at[1, step],
            recv_sem=link_sem.at[1], device_id={"slab": to_slab}, device_id_type=MESH,
        ).start()

    up_half, low_half = pl.ds(HALF, HALF), pl.ds(0, HALF)

    def halo_copy(source, halo, which, half):
        part = up_half if half else low_half
        to_slab = slab + 1 if half else slab - 1
        return pltpu.make_async_remote_copy(
            src_ref=source.at[:, part], dst_ref=halo.at[:, part],
            send_sem=halo_send.at[which, half], recv_sem=halo_recv.at[which, half],
            device_id={"slab": to_slab}, device_id_type=MESH,
        )

    def send_halo(source, halo, which):
        @pl.when(has_above)
        def _():
            halo_copy(source, halo, which, 1).start()

        @pl.when(has_below)
        def _():
            halo_copy(source, halo, which, 0).start()

    def wait_halo(source, halo, which, half):
        @pl.when(has_below if half else has_above)
        def _():
            halo_copy(source, halo, which, half).wait_recv()

    def wait_halo_send(source, halo, which):
        @pl.when(has_above)
        def _():
            halo_copy(source, halo, which, 1).wait_send()

        @pl.when(has_below)
        def _():
            halo_copy(source, halo, which, 0).wait_send()

    send_halo(f0, halo0, 0)

    if n_slab > 1:
        others = pl.ds(0, n_slab - 1)
        pltpu.make_async_copy(links_all.at[others], links_all.at[others], link_sem.at[0]).wait()
        pltpu.make_async_copy(solid_all.at[others], solid_all.at[others], link_sem.at[1]).wait()

    shape = (n_slab,) + f0.shape[2:]
    up = [links_all[:, a].astype(jnp.float32) for a in range(3)]
    at_y = lax.broadcasted_iota(jnp.int32, shape, 1)
    at_z = lax.broadcasted_iota(jnp.int32, shape, 2)
    at_x = lax.broadcasted_iota(jnp.int32, shape, 0)
    low = [
        lower(up[0]),
        jnp.where(at_y == 0, 0.0, rolled(up[1], 1, 1)),
        jnp.where(at_z == 0, 0.0, rolled(up[2], 1, 2)),
    ]
    up_in = [
        jnp.where(at_x == shape[0] - 1, 0.0, up[0]),
        jnp.where(at_y == shape[1] - 1, 0.0, up[1]),
        jnp.where(at_z == shape[2] - 1, 0.0, up[2]),
    ]
    count = up[0] + up[1] + up[2] + low[0] + low[1] + low[2]
    for a in range(3):
        faces[a] = up_in[a]
        faces[3 + a] = low[a]
    faces[6] = 1.0 / (1.0 + COUPLING * count)
    solid = solid_all[...]
    fluid = jnp.where(solid == 0, COURANT, 0.0)
    for a in range(3):
        pred[0] = fluid * low[a]
        pred[1] = fluid * up_in[a]
        pred[2] = fluid * up[a]
        coef[0, a, 0] = pred[0, slab]
        coef[0, a, 1] = pred[1, slab]
        coef[1, a, 0] = pred[2, slab]
        coef[1, a, 1] = pred[0, slab]

    coef_copy = pltpu.make_async_copy(coef, coef_out, out_sem.at[1])
    coef_copy.start()

    lead = jnp.where(has_above, 1, 0)

    def wait_dynamic(source, halo, which, half):
        @pl.when(half == 1)
        def _():
            wait_halo(source, halo, which, 1)

        @pl.when(half == 0)
        def _():
            wait_halo(source, halo, which, 0)

    def reduce_and_send(plane, source, everything, which):
        pltpu.make_async_copy(
            gather_in.at[pl.ds(0, n_vel - 1)], gather_in.at[pl.ds(0, n_vel - 1)], rs_recv
        ).wait()
        gather_in[rank] = source[plane]
        total = gather_in[0]
        for v in range(1, n_vel):
            total = total + gather_in[v]
        mine = plane * n_slab + slab
        everything[mine] = total
        for step in range(n_slab):
            to_slab = lax.rem(slab + step, n_slab)

            def one(i, _, to_slab=to_slab, step=step):
                pltpu.make_async_remote_copy(
                    src_ref=everything.at[mine], dst_ref=everything.at[mine],
                    send_sem=ag_send.at[step], recv_sem=ag_recv.at[which],
                    device_id={"slab": to_slab, "vel": lax.rem(rank + i, n_vel)}, device_id_type=MESH,
                ).start()
                return 0

            lax.fori_loop(1 if step == 0 else 0, n_vel, one, 0, unroll=5 if step == 0 else 4)

    def wait_gathered(everything, which, reduces):
        planes = MOMENTS * n_slab

        @pl.when(reduces)
        def _():
            part = everything.at[pl.ds(0, planes - 1)]
            pltpu.make_async_copy(part, part, ag_recv.at[which]).wait()

        @pl.when(jnp.logical_not(reduces))
        def _():
            pltpu.make_async_copy(everything, everything, ag_recv.at[which]).wait()

    def first_pass(half, turn):
        wait_dynamic(f0, halo0, 0, half)

        def store(j, ix, value, extra):
            base[j, ix] = value

        upwind(f0, halo0, coef, half, row_speeds, rows, store)

    first_pass(lead, 0)

    first_pass(1 - lead, 1)
    m2 = moments_of(base)
    for k in range(MOMENTS):
        send2[k] = m2[k]
    scatter(send2, first2)

    @pl.when(reduces1)
    def _():
        reduce_and_send(plane1, send1, all1, 0)

    def predict(moments):
        now = moments
        for _ in range(SWEEPS):
            beside = (
                upper(now) * faces[0] + lower(now) * faces[3]
                + rolled(now, -1, 1) * faces[1] + rolled(now, 1, 1) * faces[4]
                + rolled(now, -1, 2) * faces[2] + rolled(now, 1, 2) * faces[5]
            )
            now = (moments + COUPLING * beside) * faces[6]
        return now

    @pl.when(reduces2)
    def _():
        reduce_and_send(plane2, send2, all2, 1)

    wait_gathered(all1, 0, reduces1)
    state1 = [predict(all1[k * n_slab:(k + 1) * n_slab]) for k in range(MOMENTS)]
    u, per_temp, s, inv, amp = masked_state(state1, solid)

    def own(planes):
        for k, plane in enumerate(planes):
            pred[k] = plane
        return [pred[k, slab] for k in range(len(planes))]

    near = own([*u, per_temp, *s, inv]) + own([amp])
    fill_bells(gx, near)

    def relax_rows(half):
        def one(j, carry):
            y, z = row_speeds(j)
            extra = bell_row(near, speed_of(y), speed_of(z))
            for i in range(HALF):
                ix = half * HALF + i
                base[j, ix] = relaxed(gx, near, ix, base[j, ix], extra)
            return carry

        lax.fori_loop(0, rows, one, 0, unroll=math.gcd(4, rows))

    relax_rows(lead)

    @pl.when(lead == 1)
    def _():
        @pl.when(has_above)
        def _():
            halo_copy(base, halo1, 1, 1).start()

    @pl.when(lead == 0)
    def _():
        @pl.when(has_below)
        def _():
            halo_copy(base, halo1, 1, 0).start()

    relax_rows(1 - lead)
    base_copy = pltpu.make_async_copy(base, base_out, out_sem.at[0])
    base_copy.start()

    @pl.when(jnp.logical_and(lead == 1, has_below))
    def _():
        halo_copy(base, halo1, 1, 0).start()

    target = goal_moments(u, per_temp, s, amp)

    wait_gathered(all2, 1, reduces2)
    state2 = [
        predict(all2[k * n_slab:(k + 1) * n_slab] * inv + target[k]) for k in range(MOMENTS)
    ]
    u, per_temp, s, inv, amp = masked_state(state2, solid)
    for k, plane in enumerate(own([*u, per_temp, *s, inv]) + own([amp])):
        state[k] = plane
    state_copy = pltpu.make_async_copy(state, state_out, out_sem.at[2])
    state_copy.start()

    for half in range(2):
        wait_halo(base, halo1, 1, half)

        @pl.when(jnp.logical_not(has_below if half else has_above))
        def _():
            zero_copy(half * HALF).wait()

    wait_halo_send(f0, halo0, 0)
    wait_halo_send(base, halo1, 1)
    for step in range(1, n_slab):
        pltpu.make_async_copy(links_all.at[0], links_all.at[0], link_send.at[0, step]).wait()
        pltpu.make_async_copy(solid_all.at[0], solid_all.at[0], link_send.at[1, step]).wait()
    for which, reduces in ((0, reduces1), (1, reduces2)):
        source = send1 if which == 0 else send2

        @pl.when(reduces)
        def _():
            part = source.at[pl.ds(0, MOMENTS - 1)]
            pltpu.make_async_copy(part, part, rs_send.at[which]).wait()
            for step in range(n_slab):
                part = gather_in.at[pl.ds(0, n_vel - 1 if step == 0 else n_vel)]
                pltpu.make_async_copy(part, part, ag_send.at[step]).wait()

        @pl.when(jnp.logical_not(reduces))
        def _():
            pltpu.make_async_copy(source, source, rs_send.at[which]).wait()

    for copy in (base_copy, coef_copy, state_copy):
        copy.wait()


def body(f_start, links, solid):
    n_slab, n_vel = lax.axis_size("slab"), lax.axis_size("vel")
    vel_local, planes = f_start.shape[:2]
    cells = f_start.shape[2:]
    rows = vel_local // NQ
    assert planes == 1 and rows * NQ == vel_local and rows % 2 == 0 and n_vel >= 2 * MOMENTS
    f32, vmem, dma = jnp.float32, pltpu.VMEM, pltpu.SemaphoreType.DMA
    block = (rows, NQ) + cells
    grid = (n_slab,) + cells
    any_spec = pl.BlockSpec(memory_space=pltpu.HBM)
    base, halo, state, coef = pl.pallas_call(
        functools.partial(kernel, n_slab, n_vel),
        out_shape=[
            jax.ShapeDtypeStruct(block, f32), jax.ShapeDtypeStruct(block, f32),
            jax.ShapeDtypeStruct((9,) + cells, f32), jax.ShapeDtypeStruct((2, 3, 2) + cells, f32),
        ],
        in_specs=[any_spec] * 3,
        out_specs=[any_spec] * 4,
        scratch_shapes=[
            vmem(block, f32), vmem(block, f32), vmem(block, f32), vmem((9,) + cells, f32),
            vmem((n_slab, 3) + cells, jnp.int32), vmem(grid, jnp.int32),
            vmem((MOMENTS,) + cells, f32), vmem((MOMENTS,) + cells, f32),
            vmem((n_vel,) + cells, f32),
            vmem((MOMENTS * n_slab,) + cells, f32), vmem((MOMENTS * n_slab,) + cells, f32),
            vmem((7,) + grid, f32), vmem((2, 3, 2) + cells, f32), vmem((3, NQ) + cells, f32),
            vmem((MOMENTS,) + grid, f32),
            dma((3,)), dma((2,)), dma((2, n_slab)), dma((2, 2)), dma((2, 2)), dma, dma((2,)),
            dma((2,)), dma((n_slab,)), dma((3,)), dma((2,)),
        ],
        compiler_params=pltpu.CompilerParams(
            collective_id=0, has_side_effects=True, vmem_limit_bytes=60 * 1024 * 1024
        ),
    )(f_start.reshape(block), links.reshape((3,) + cells), solid.reshape(cells))
    pieces = math.gcd(4, rows)
    piece = pl.BlockSpec((rows // pieces, NQ) + cells, lambda i: (i, 0, 0, 0))
    out = pl.pallas_call(
        functools.partial(last_kernel, rows),
        grid=(pieces,),
        out_shape=jax.ShapeDtypeStruct(block, f32),
        in_specs=[
            piece, piece,
            pl.BlockSpec((9,) + cells, lambda i: (0, 0, 0)),
            pl.BlockSpec((2, 3, 2) + cells, lambda i: (0, 0, 0, 0, 0)),
        ],
        out_specs=piece,
        scratch_shapes=[vmem((3, NQ) + cells, f32)],
        compiler_params=pltpu.CompilerParams(vmem_limit_bytes=60 * 1024 * 1024),
    )(base, halo, state, coef)
    return out.reshape(f_start.shape)


def solution(mesh):
    in_specs = (P("vel", "slab", None, None), P(None, "slab", None, None), P("slab", None, None))
    out_specs = P("vel", "slab", None, None)
    return jax.shard_map(body, mesh=mesh, in_specs=in_specs, out_specs=out_specs, check_vma=False)
```

```python
import functools
import math

import jax
import jax.numpy as jnp
from jax import lax
from jax.experimental import pallas as pl
from jax.experimental.pallas import tpu as pltpu
from jax.sharding import PartitionSpec as P

NQ = 16
HALF = NQ // 2
SWEEPS = 2
MOMENTS = 8

SPACING = 0.6
COUPLING = 1.0
COURANT = 0.06
RELAXATION_FREQ = 0.5
VISCOUS_TO_HEAT = 2.0 / 3.0
QUAD_WEIGHT = SPACING**3 / (2.0 * math.pi) ** 1.5

MESH = pl.DeviceIdType.MESH


def speed_of(index):
    return (index.astype(jnp.float32) - (NQ - 1) / 2.0) * SPACING


def rolled(cells, shift, axis):
    size = cells.shape[axis]
    return pltpu.roll(cells, shift % size if isinstance(shift, int) else shift, axis)


def upper(cells):
    return jnp.concatenate([cells[1:], jnp.zeros_like(cells[:1])], axis=0)


def lower(cells):
    return jnp.concatenate([jnp.zeros_like(cells[:1]), cells[:-1]], axis=0)


def macro_state(predicted):
    rho = predicted[0]
    per_rho = 1.0 / rho
    u = [predicted[1 + a] * per_rho for a in range(3)]
    energy = predicted[4]
    temp = (2.0 * energy * per_rho - (u[0] * u[0] + u[1] * u[1] + u[2] * u[2])) / 3.0
    pressure = rho * temp
    nu = RELAXATION_FREQ * rho * jnp.exp(0.28 * jnp.log(temp))
    scale = (1.0 - VISCOUS_TO_HEAT) / (5.0 * pressure * temp)
    s = [(predicted[5 + a] - u[a] * (energy + pressure)) * scale for a in range(3)]
    root = lax.rsqrt(temp)
    return u, temp, nu, s, rho * (root * root * root)


def masked_state(predicted, solid):
    u, temp, nu, s, height = macro_state(predicted)
    fluid = solid == 0
    per_temp = jnp.where(fluid, 1.0 / temp, 1.0)
    u = [jnp.where(fluid, x, 0.0) for x in u]
    s = [jnp.where(fluid, x, 0.0) for x in s]
    inv = jnp.where(fluid, 1.0 / (1.0 + nu), 1.0)
    amp = jnp.where(fluid, height * (nu / (1.0 + nu)), 0.0)
    return u, per_temp, s, inv, amp


def goal_moments(u, per_temp, s, amp):
    def one(i, sums):
        xi = speed_of(i)
        new = []
        for a in range(3):
            c = xi - u[a]
            term = jnp.exp(-0.5 * (c * c * per_temp))
            row = [sums[a][0] + term]
            for k in range(1, 7):
                term = term * c
                row.append(sums[a][k] + term)
            new.append(tuple(row))
        return tuple(new)

    zero = jnp.zeros_like(per_temp)
    line = lax.fori_loop(0, NQ, one, tuple((zero,) * 7 for _ in range(3)), unroll=4)
    pairs, products, heats, lifts = {}, {}, {}, {}

    def add(m, a, n=1):
        return tuple(k + n * (a == d) for d, k in enumerate(m))

    def f(m):
        if m not in products:
            if m[:2] not in pairs:
                pairs[m[:2]] = line[0][m[0]] * line[1][m[1]]
            products[m] = pairs[m[:2]] * line[2][m[2]]
        return products[m]

    def q(m):
        if m not in heats:
            heats[m] = f(add(m, 0, 2)) + f(add(m, 1, 2)) + f(add(m, 2, 2))
        return heats[m]

    def lift(m):
        if m not in lifts:
            lifts[m] = per_temp * q(m) - 5.0 * f(m)
        return lifts[m]

    def total(m):
        out = f(m)
        for a in range(3):
            out = out + s[a] * lift(add(m, a))
        return out

    def total_q(m):
        out = q(m)
        for a in range(3):
            up = add(m, a)
            out = out + s[a] * (lift(add(up, 0, 2)) + lift(add(up, 1, 2)) + lift(add(up, 2, 2)))
        return out

    origin = (0, 0, 0)
    weight = amp * QUAD_WEIGHT
    p0 = total(origin) * weight
    p1 = [total(add(origin, a)) * weight for a in range(3)]
    p2 = {}
    for a in range(3):
        for b in range(a, 3):
            p2[a, b] = p2[b, a] = total(add(add(origin, a), b)) * weight
    p3 = [total_q(add(origin, a)) * weight for a in range(3)]
    half_uu = 0.5 * (u[0] * u[0] + u[1] * u[1] + u[2] * u[2])
    energy = (
        0.5 * (p2[0, 0] + p2[1, 1] + p2[2, 2])
        + (u[0] * p1[0] + u[1] * p1[1] + u[2] * p1[2])
        + half_uu * p0
    )
    out = [p0] + [p1[a] + u[a] * p0 for a in range(3)] + [energy]
    for a in range(3):
        out.append(
            0.5 * p3[a]
            + (u[0] * p2[a, 0] + u[1] * p2[a, 1] + u[2] * p2[a, 2])
            + half_uu * p1[a]
            + u[a] * energy
        )
    return out


def kernel(
    n_slab, n_vel, f_ref, links_ref, solid_ref, out_ref,
    f0, base, halo0, halo1, links_all, solid_all, send1, send2, gather_in, all1, all2,
    faces, coef, gx, pred,
    load_sem, link_sem, link_send, halo_recv, halo_send, rs_recv, rs_send, ag_recv, ag_send,
):
    slab = lax.axis_index("slab")
    rank = lax.axis_index("vel")
    rows = f_ref.shape[0]
    first1 = n_vel // 2 - MOMENTS // 2
    first2 = n_vel // 2 + MOMENTS // 2
    plane1 = rank - first1
    plane2 = lax.rem(rank - first2 + n_vel, n_vel)
    reduces1 = (plane1 >= 0) & (plane1 < MOMENTS)
    reduces2 = plane2 < MOMENTS
    has_below = slab > 0
    has_above = slab < n_slab - 1

    def start_all(copies):
        for copy in copies:
            copy.start()

    loads = [
        pltpu.make_async_copy(f_ref, f0, load_sem.at[0]),
        pltpu.make_async_copy(links_ref, links_all.at[slab], load_sem.at[1]),
        pltpu.make_async_copy(solid_ref, solid_all.at[slab], load_sem.at[2]),
    ]
    start_all(loads)

    barrier = pltpu.get_barrier_semaphore()
    for step in range(n_slab):
        to_slab = lax.rem(slab + step, n_slab)

        def greet(i, _, to_slab=to_slab):
            pl.semaphore_signal(
                barrier, inc=1, device_id={"slab": to_slab, "vel": lax.rem(rank + i, n_vel)},
                device_id_type=MESH,
            )
            return 0

        lax.fori_loop(1 if step == 0 else 0, n_vel, greet, 0, unroll=5 if step == 0 else 4)

    def clear(low):
        def one(j, _):
            for i in range(HALF):
                zero = jnp.zeros(f0.shape[2:], jnp.float32)
                halo0[j, low + i] = zero
                halo1[j, low + i] = zero
            return 0

        lax.fori_loop(0, rows, one, 0)

    @pl.when(jnp.logical_not(has_below))
    def _():
        clear(HALF)

    @pl.when(jnp.logical_not(has_above))
    def _():
        clear(0)

    def row_speeds(j):
        row = rank * rows + j
        return lax.rem(row, NQ), lax.div(row, NQ)

    def add_row(sums, a0, a1, a2, a3, xi_y, xi_z):
        r = xi_y * xi_y + xi_z * xi_z
        e = 0.5 * (a2 + r * a0)
        return (
            sums[0] + a0, sums[1] + a1, sums[2] + xi_y * a0, sums[3] + xi_z * a0,
            sums[4] + e, sums[5] + 0.5 * (a3 + r * a1), sums[6] + xi_y * e, sums[7] + xi_z * e,
        )

    def moments_of(source):
        def one(j, sums):
            y, z = row_speeds(j)
            a0 = a1 = a2 = a3 = None
            for i in range(HALF):
                xi = (i + 0.5) * SPACING
                plus, minus = source[j, HALF + i], source[j, HALF - 1 - i]
                even, odd = plus + minus, plus - minus
                t = [even * QUAD_WEIGHT, odd * (QUAD_WEIGHT * xi),
                     even * (QUAD_WEIGHT * xi**2), odd * (QUAD_WEIGHT * xi**3)]
                if i == 0:
                    a0, a1, a2, a3 = t
                else:
                    a0, a1, a2, a3 = a0 + t[0], a1 + t[1], a2 + t[2], a3 + t[3]
            return add_row(sums, a0, a1, a2, a3, speed_of(y), speed_of(z))

        zero = jnp.zeros(f0.shape[2:], jnp.float32)
        return lax.fori_loop(0, rows, one, (zero,) * MOMENTS, unroll=2)

    loads[0].wait()
    m1 = moments_of(f0)
    for k in range(MOMENTS):
        send1[k] = m1[k]
    loads[1].wait()
    loads[2].wait()
    pl.semaphore_wait(barrier, n_slab * n_vel - 1)

    def scatter(source, first):
        def one(i, _):
            k = lax.rem(rank + i, MOMENTS)
            target = lax.rem(first + k, n_vel)

            @pl.when(target != rank)
            def _():
                pltpu.make_async_remote_copy(
                    src_ref=source.at[k], dst_ref=gather_in.at[rank],
                    send_sem=rs_send.at[0 if source is send1 else 1], recv_sem=rs_recv,
                    device_id={"vel": target}, device_id_type=MESH,
                ).start()

            return 0

        lax.fori_loop(0, MOMENTS, one, 0, unroll=True)

    scatter(send1, first1)

    for step in range(1, n_slab):
        to_slab = lax.rem(slab + step, n_slab)
        pltpu.make_async_remote_copy(
            src_ref=links_ref, dst_ref=links_all.at[slab], send_sem=link_send.at[0, step],
            recv_sem=link_sem.at[0], device_id={"slab": to_slab}, device_id_type=MESH,
        ).start()
        pltpu.make_async_remote_copy(
            src_ref=solid_ref, dst_ref=solid_all.at[slab], send_sem=link_send.at[1, step],
            recv_sem=link_sem.at[1], device_id={"slab": to_slab}, device_id_type=MESH,
        ).start()

    up_half, low_half = pl.ds(HALF, HALF), pl.ds(0, HALF)

    def halo_copy(source, halo, which, half):
        part = up_half if half else low_half
        to_slab = slab + 1 if half else slab - 1
        return pltpu.make_async_remote_copy(
            src_ref=source.at[:, part], dst_ref=halo.at[:, part],
            send_sem=halo_send.at[which, half], recv_sem=halo_recv.at[which, half],
            device_id={"slab": to_slab}, device_id_type=MESH,
        )

    def send_halo(source, halo, which):
        @pl.when(has_above)
        def _():
            halo_copy(source, halo, which, 1).start()

        @pl.when(has_below)
        def _():
            halo_copy(source, halo, which, 0).start()

    def wait_halo(source, halo, which, half):
        @pl.when(has_below if half else has_above)
        def _():
            halo_copy(source, halo, which, half).wait_recv()

    def wait_halo_send(source, halo, which):
        @pl.when(has_above)
        def _():
            halo_copy(source, halo, which, 1).wait_send()

        @pl.when(has_below)
        def _():
            halo_copy(source, halo, which, 0).wait_send()

    send_halo(f0, halo0, 0)

    if n_slab > 1:
        others = pl.ds(0, n_slab - 1)
        pltpu.make_async_copy(links_all.at[others], links_all.at[others], link_sem.at[0]).wait()
        pltpu.make_async_copy(solid_all.at[others], solid_all.at[others], link_sem.at[1]).wait()

    shape = (n_slab,) + f0.shape[2:]
    up = [links_all[:, a].astype(jnp.float32) for a in range(3)]
    at_y = lax.broadcasted_iota(jnp.int32, shape, 1)
    at_z = lax.broadcasted_iota(jnp.int32, shape, 2)
    at_x = lax.broadcasted_iota(jnp.int32, shape, 0)
    low = [
        lower(up[0]),
        jnp.where(at_y == 0, 0.0, rolled(up[1], 1, 1)),
        jnp.where(at_z == 0, 0.0, rolled(up[2], 1, 2)),
    ]
    up_in = [
        jnp.where(at_x == shape[0] - 1, 0.0, up[0]),
        jnp.where(at_y == shape[1] - 1, 0.0, up[1]),
        jnp.where(at_z == shape[2] - 1, 0.0, up[2]),
    ]
    count = up[0] + up[1] + up[2] + low[0] + low[1] + low[2]
    for a in range(3):
        faces[a] = up_in[a]
        faces[3 + a] = low[a]
    faces[6] = 1.0 / (1.0 + COUPLING * count)
    solid = solid_all[...]
    fluid = jnp.where(solid == 0, COURANT, 0.0)
    for a in range(3):
        pred[0] = fluid * low[a]
        pred[1] = fluid * up_in[a]
        pred[2] = fluid * up[a]
        coef[0, a, 0] = pred[0, slab]
        coef[0, a, 1] = pred[1, slab]
        coef[1, a, 0] = pred[2, slab]
        coef[1, a, 1] = pred[0, slab]

    def streamed(source, halo, half, first_row, row_end, finish):
        cells = f0.shape[2:]
        abs_of = [jnp.abs(speed_of(half * HALF + i)) for i in range(HALF)]

        def one(j, carry):
            y, z = row_speeds(j)
            xi_y, xi_z = speed_of(y), speed_of(z)
            sign_y = jnp.where(y >= HALF, 1, 0)
            sign_z = jnp.where(z >= HALF, 1, 0)
            turn_y = jnp.where(y >= HALF, 1, cells[0] - 1)
            turn_z = jnp.where(z >= HALF, 1, cells[1] - 1)
            abs_y, abs_z = jnp.abs(xi_y), jnp.abs(xi_z)
            stay = 1.0 - (abs_y * coef[sign_y, 1, 0] + abs_z * coef[sign_z, 2, 0])
            in_y = abs_y * coef[sign_y, 1, 1]
            in_z = abs_z * coef[sign_z, 2, 1]
            out_x, in_x = coef[half, 0, 0], coef[half, 0, 1]
            extra = finish.row(j, xi_y, xi_z) if finish else None
            for i in range(HALF):
                ix = half * HALF + i
                abs_x = abs_of[i]
                f = source[j, ix]
                value = (
                    f * (stay - abs_x * out_x)
                    + in_y * rolled(f, turn_y, 0)
                    + in_z * rolled(f, turn_z, 1)
                    + abs_x * (in_x * halo[j, ix])
                )
                if finish:
                    finish.store(j, ix, value, extra)
                else:
                    base[j, ix] = value
            return carry

        lax.fori_loop(first_row, row_end, one, 0, unroll=math.gcd(4, row_end - first_row))

    class Goal:
        def __init__(self, target, u, per_temp, s, inv, amp):
            self.target, self.u, self.per_temp, self.s, self.inv, self.amp = target, u, per_temp, s, inv, amp

            def one(i, _):
                c = speed_of(i) - u[0]
                part = c * c * per_temp
                gx[0, i] = jnp.exp(-0.5 * part)
                gx[1, i] = s[0] * c
                gx[2, i] = part
                return 0

            lax.fori_loop(0, NQ, one, 0, unroll=4)

        def row(self, j, xi_y, xi_z):
            c_y, c_z = xi_y - self.u[1], xi_z - self.u[2]
            part = (c_y * c_y + c_z * c_z) * self.per_temp
            return jnp.exp(-0.5 * part) * self.amp, self.s[1] * c_y + self.s[2] * c_z, part - 5.0

        def store(self, j, ix, value, extra):
            height, along, part = extra
            bell = gx[0, ix] * height
            self.target[j, ix] = value * self.inv + bell * (1.0 + (gx[1, ix] + along) * (gx[2, ix] + part))

    lead = jnp.where(has_above, 1, 0)

    def both_halves(body):
        for turn in range(2):
            body(lead if turn == 0 else 1 - lead, turn)

    def wait_dynamic(source, halo, which, half):
        @pl.when(half == 1)
        def _():
            wait_halo(source, halo, which, 1)

        @pl.when(half == 0)
        def _():
            wait_halo(source, halo, which, 0)

    def reduce_and_send(plane, source, everything, which):
        pltpu.make_async_copy(
            gather_in.at[pl.ds(0, n_vel - 1)], gather_in.at[pl.ds(0, n_vel - 1)], rs_recv
        ).wait()
        gather_in[rank] = source[plane]
        total = gather_in[0]
        for v in range(1, n_vel):
            total = total + gather_in[v]
        mine = plane * n_slab + slab
        everything[mine] = total
        for step in range(n_slab):
            to_slab = lax.rem(slab + step, n_slab)

            def one(i, _, to_slab=to_slab, step=step):
                pltpu.make_async_remote_copy(
                    src_ref=everything.at[mine], dst_ref=everything.at[mine],
                    send_sem=ag_send.at[step], recv_sem=ag_recv.at[which],
                    device_id={"slab": to_slab, "vel": lax.rem(rank + i, n_vel)}, device_id_type=MESH,
                ).start()
                return 0

            lax.fori_loop(1 if step == 0 else 0, n_vel, one, 0, unroll=5 if step == 0 else 4)

    def wait_gathered(everything, which, reduces):
        planes = MOMENTS * n_slab

        @pl.when(reduces)
        def _():
            part = everything.at[pl.ds(0, planes - 1)]
            pltpu.make_async_copy(part, part, ag_recv.at[which]).wait()

        @pl.when(jnp.logical_not(reduces))
        def _():
            pltpu.make_async_copy(everything, everything, ag_recv.at[which]).wait()

    def first_pass(half, turn):
        wait_dynamic(f0, halo0, 0, half)
        streamed(f0, halo0, half, 0, rows, None)

    first_pass(lead, 0)

    first_pass(1 - lead, 1)
    m2 = moments_of(base)
    for k in range(MOMENTS):
        send2[k] = m2[k]
    scatter(send2, first2)

    @pl.when(reduces1)
    def _():
        reduce_and_send(plane1, send1, all1, 0)

    def predict(moments):
        now = moments
        for _ in range(SWEEPS):
            beside = (
                upper(now) * faces[0] + lower(now) * faces[3]
                + rolled(now, -1, 1) * faces[1] + rolled(now, 1, 1) * faces[4]
                + rolled(now, -1, 2) * faces[2] + rolled(now, 1, 2) * faces[5]
            )
            now = (moments + COUPLING * beside) * faces[6]
        return now

    @pl.when(reduces2)
    def _():
        reduce_and_send(plane2, send2, all2, 1)

    wait_gathered(all1, 0, reduces1)
    state1 = [predict(all1[k * n_slab:(k + 1) * n_slab]) for k in range(MOMENTS)]
    u, per_temp, s, inv, amp = masked_state(state1, solid)

    def own(planes):
        for k, plane in enumerate(planes):
            pred[k] = plane
        return [pred[k, slab] for k in range(len(planes))]

    near = own([*u, per_temp, *s, inv])
    near_amp = own([amp])[0]
    goal = Goal(base, near[0:3], near[3], near[4:7], near[7], near_amp)

    def relax_rows(half):
        def one(j, carry):
            y, z = row_speeds(j)
            extra = goal.row(j, speed_of(y), speed_of(z))
            for i in range(HALF):
                goal.store(j, half * HALF + i, base[j, half * HALF + i], extra)
            return carry

        lax.fori_loop(0, rows, one, 0, unroll=math.gcd(4, rows))

    relax_rows(lead)

    @pl.when(lead == 1)
    def _():
        @pl.when(has_above)
        def _():
            halo_copy(base, halo1, 1, 1).start()

    @pl.when(lead == 0)
    def _():
        @pl.when(has_below)
        def _():
            halo_copy(base, halo1, 1, 0).start()

    relax_rows(1 - lead)

    @pl.when(jnp.logical_and(lead == 1, has_below))
    def _():
        halo_copy(base, halo1, 1, 0).start()

    target = goal_moments(u, per_temp, s, amp)

    wait_gathered(all2, 1, reduces2)
    state2 = [
        predict(all2[k * n_slab:(k + 1) * n_slab] * inv + target[k]) for k in range(MOMENTS)
    ]
    u, per_temp, s, inv, amp = masked_state(state2, solid)
    near = own([*u, per_temp, *s, inv])
    near_amp = own([amp])[0]
    final = Goal(out_ref, near[0:3], near[3], near[4:7], near[7], near_amp)

    def last_pass(half, turn):
        wait_dynamic(base, halo1, 1, half)
        streamed(base, halo1, half, 0, rows, final)

    both_halves(last_pass)

    wait_halo_send(f0, halo0, 0)
    wait_halo_send(base, halo1, 1)
    for step in range(1, n_slab):
        pltpu.make_async_copy(links_all.at[0], links_all.at[0], link_send.at[0, step]).wait()
        pltpu.make_async_copy(solid_all.at[0], solid_all.at[0], link_send.at[1, step]).wait()
    for which, reduces in ((0, reduces1), (1, reduces2)):
        source = send1 if which == 0 else send2

        @pl.when(reduces)
        def _():
            part = source.at[pl.ds(0, MOMENTS - 1)]
            pltpu.make_async_copy(part, part, rs_send.at[which]).wait()
            for step in range(n_slab):
                part = gather_in.at[pl.ds(0, n_vel - 1 if step == 0 else n_vel)]
                pltpu.make_async_copy(part, part, ag_send.at[step]).wait()

        @pl.when(jnp.logical_not(reduces))
        def _():
            pltpu.make_async_copy(source, source, rs_send.at[which]).wait()


def body(f_start, links, solid):
    n_slab, n_vel = lax.axis_size("slab"), lax.axis_size("vel")
    vel_local, planes = f_start.shape[:2]
    cells = f_start.shape[2:]
    rows = vel_local // NQ
    assert planes == 1 and rows * NQ == vel_local and rows % 2 == 0 and n_vel >= 2 * MOMENTS
    f32, vmem, dma = jnp.float32, pltpu.VMEM, pltpu.SemaphoreType.DMA
    block = (rows, NQ) + cells
    grid = (n_slab,) + cells
    any_spec = pl.BlockSpec(memory_space=pltpu.HBM)
    out = pl.pallas_call(
        functools.partial(kernel, n_slab, n_vel),
        out_shape=jax.ShapeDtypeStruct(block, f32),
        in_specs=[any_spec] * 3,
        out_specs=pl.BlockSpec(memory_space=pltpu.VMEM),
        scratch_shapes=[
            vmem(block, f32), vmem(block, f32), vmem(block, f32), vmem(block, f32),
            vmem((n_slab, 3) + cells, jnp.int32), vmem(grid, jnp.int32),
            vmem((MOMENTS,) + cells, f32), vmem((MOMENTS,) + cells, f32),
            vmem((n_vel,) + cells, f32),
            vmem((MOMENTS * n_slab,) + cells, f32), vmem((MOMENTS * n_slab,) + cells, f32),
            vmem((7,) + grid, f32), vmem((2, 3, 2) + cells, f32), vmem((3, NQ) + cells, f32),
            vmem((MOMENTS,) + grid, f32),
            dma((3,)), dma((2,)), dma((2, n_slab)), dma((2, 2)), dma((2, 2)), dma, dma((2,)),
            dma((2,)), dma((n_slab,)),
        ],
        compiler_params=pltpu.CompilerParams(
            collective_id=0, has_side_effects=True, vmem_limit_bytes=32 * 1024 * 1024
        ),
    )(*(
        pltpu.with_memory_space_constraint(x, pltpu.HBM)
        for x in (f_start.reshape(block), links.reshape((3,) + cells), solid.reshape(cells))
    ))
    return out.reshape(f_start.shape)


def solution(mesh):
    in_specs = (P("vel", "slab", None, None), P(None, "slab", None, None), P("slab", None, None))
    out_specs = P("vel", "slab", None, None)
    return jax.shard_map(body, mesh=mesh, in_specs=in_specs, out_specs=out_specs, check_vma=False)
```

```python
import functools
import math

import jax
import jax.numpy as jnp
from jax import lax
from jax.experimental import pallas as pl
from jax.experimental.pallas import tpu as pltpu
from jax.sharding import PartitionSpec as P

NQ = 16
HALF = NQ // 2
SWEEPS = 2
MOMENTS = 8

SPACING = 0.6
COUPLING = 1.0
COURANT = 0.06
RELAXATION_FREQ = 0.5
VISCOUS_TO_HEAT = 2.0 / 3.0
QUAD_WEIGHT = SPACING**3 / (2.0 * math.pi) ** 1.5

MESH = pl.DeviceIdType.MESH


def speed_of(index):
    return (index.astype(jnp.float32) - (NQ - 1) / 2.0) * SPACING


def rolled(cells, shift, axis):
    size = cells.shape[axis]
    return pltpu.roll(cells, shift % size if isinstance(shift, int) else shift, axis)


def upper(cells):
    return jnp.concatenate([cells[1:], jnp.zeros_like(cells[:1])], axis=0)


def lower(cells):
    return jnp.concatenate([jnp.zeros_like(cells[:1]), cells[:-1]], axis=0)


def macro_state(predicted):
    rho = predicted[0]
    per_rho = 1.0 / rho
    u = [predicted[1 + a] * per_rho for a in range(3)]
    energy = predicted[4]
    temp = (2.0 * energy * per_rho - (u[0] * u[0] + u[1] * u[1] + u[2] * u[2])) / 3.0
    pressure = rho * temp
    nu = RELAXATION_FREQ * rho * jnp.exp(0.28 * jnp.log(temp))
    scale = (1.0 - VISCOUS_TO_HEAT) / (5.0 * pressure * temp)
    s = [(predicted[5 + a] - u[a] * (energy + pressure)) * scale for a in range(3)]
    root = lax.rsqrt(temp)
    return u, temp, nu, s, rho * (root * root * root)


def masked_state(predicted, solid):
    u, temp, nu, s, height = macro_state(predicted)
    fluid = solid == 0
    per_temp = jnp.where(fluid, 1.0 / temp, 1.0)
    u = [jnp.where(fluid, x, 0.0) for x in u]
    s = [jnp.where(fluid, x, 0.0) for x in s]
    inv = jnp.where(fluid, 1.0 / (1.0 + nu), 1.0)
    amp = jnp.where(fluid, height * (nu / (1.0 + nu)), 0.0)
    return u, per_temp, s, inv, amp


def goal_moments(u, per_temp, s, amp):
    def one(i, sums):
        xi = speed_of(i)
        new = []
        for a in range(3):
            c = xi - u[a]
            term = jnp.exp(-0.5 * (c * c * per_temp))
            row = [sums[a][0] + term]
            for k in range(1, 7):
                term = term * c
                row.append(sums[a][k] + term)
            new.append(tuple(row))
        return tuple(new)

    zero = jnp.zeros_like(per_temp)
    line = lax.fori_loop(0, NQ, one, tuple((zero,) * 7 for _ in range(3)), unroll=4)
    pairs, products, heats, lifts = {}, {}, {}, {}

    def add(m, a, n=1):
        return tuple(k + n * (a == d) for d, k in enumerate(m))

    def f(m):
        if m not in products:
            if m[:2] not in pairs:
                pairs[m[:2]] = line[0][m[0]] * line[1][m[1]]
            products[m] = pairs[m[:2]] * line[2][m[2]]
        return products[m]

    def q(m):
        if m not in heats:
            heats[m] = f(add(m, 0, 2)) + f(add(m, 1, 2)) + f(add(m, 2, 2))
        return heats[m]

    def lift(m):
        if m not in lifts:
            lifts[m] = per_temp * q(m) - 5.0 * f(m)
        return lifts[m]

    def total(m):
        out = f(m)
        for a in range(3):
            out = out + s[a] * lift(add(m, a))
        return out

    def total_q(m):
        out = q(m)
        for a in range(3):
            up = add(m, a)
            out = out + s[a] * (lift(add(up, 0, 2)) + lift(add(up, 1, 2)) + lift(add(up, 2, 2)))
        return out

    origin = (0, 0, 0)
    weight = amp * QUAD_WEIGHT
    p0 = total(origin) * weight
    p1 = [total(add(origin, a)) * weight for a in range(3)]
    p2 = {}
    for a in range(3):
        for b in range(a, 3):
            p2[a, b] = p2[b, a] = total(add(add(origin, a), b)) * weight
    p3 = [total_q(add(origin, a)) * weight for a in range(3)]
    half_uu = 0.5 * (u[0] * u[0] + u[1] * u[1] + u[2] * u[2])
    energy = (
        0.5 * (p2[0, 0] + p2[1, 1] + p2[2, 2])
        + (u[0] * p1[0] + u[1] * p1[1] + u[2] * p1[2])
        + half_uu * p0
    )
    out = [p0] + [p1[a] + u[a] * p0 for a in range(3)] + [energy]
    for a in range(3):
        out.append(
            0.5 * p3[a]
            + (u[0] * p2[a, 0] + u[1] * p2[a, 1] + u[2] * p2[a, 2])
            + half_uu * p1[a]
            + u[a] * energy
        )
    return out


def kernel(
    n_slab, n_vel, f_ref, links_ref, solid_ref, out_ref,
    f0, base, halo0, halo1, links_all, solid_all, send1, send2, gather_in, all1, all2,
    faces, coef, gx, pred,
    f_sem, load_sem, link_sem, link_send, halo_recv, halo_send, rs_recv, rs_send, ag_recv, ag_send,
):
    slab = lax.axis_index("slab")
    rank = lax.axis_index("vel")
    rows = f_ref.shape[0]
    chunks = math.gcd(4, rows)
    size = rows // chunks
    first1 = n_vel // 2 - MOMENTS // 2
    first2 = n_vel // 2 + MOMENTS // 2
    plane1 = rank - first1
    plane2 = lax.rem(rank - first2 + n_vel, n_vel)
    reduces1 = (plane1 >= 0) & (plane1 < MOMENTS)
    reduces2 = plane2 < MOMENTS
    has_below = slab > 0
    has_above = slab < n_slab - 1

    def start_all(copies):
        for copy in copies:
            copy.start()

    loads = [
        pltpu.make_async_copy(links_ref, links_all.at[slab], load_sem.at[0]),
        pltpu.make_async_copy(solid_ref, solid_all.at[slab], load_sem.at[1]),
    ]
    pieces = [pl.ds(c * size, size) for c in range(chunks)]
    f_loads = [pltpu.make_async_copy(f_ref.at[p], f0.at[p], f_sem.at[c]) for c, p in enumerate(pieces)]
    start_all(f_loads + loads)

    barrier = pltpu.get_barrier_semaphore()
    for step in range(n_slab):
        to_slab = lax.rem(slab + step, n_slab)

        def greet(i, _, to_slab=to_slab):
            pl.semaphore_signal(
                barrier, inc=1, device_id={"slab": to_slab, "vel": lax.rem(rank + i, n_vel)},
                device_id_type=MESH,
            )
            return 0

        lax.fori_loop(1 if step == 0 else 0, n_vel, greet, 0, unroll=5 if step == 0 else 4)

    def clear(low):
        def one(j, _):
            for i in range(HALF):
                zero = jnp.zeros(f0.shape[2:], jnp.float32)
                halo0[j, low + i] = zero
                halo1[j, low + i] = zero
            return 0

        lax.fori_loop(0, rows, one, 0)

    @pl.when(jnp.logical_not(has_below))
    def _():
        clear(HALF)

    @pl.when(jnp.logical_not(has_above))
    def _():
        clear(0)

    def row_speeds(j):
        row = rank * rows + j
        return lax.rem(row, NQ), lax.div(row, NQ)

    def add_row(sums, a0, a1, a2, a3, xi_y, xi_z):
        r = xi_y * xi_y + xi_z * xi_z
        e = 0.5 * (a2 + r * a0)
        return (
            sums[0] + a0, sums[1] + a1, sums[2] + xi_y * a0, sums[3] + xi_z * a0,
            sums[4] + e, sums[5] + 0.5 * (a3 + r * a1), sums[6] + xi_y * e, sums[7] + xi_z * e,
        )

    def moments_of(source, ready=None):
        def one(j, sums):
            y, z = row_speeds(j)
            a0 = a1 = a2 = a3 = None
            for i in range(HALF):
                xi = (i + 0.5) * SPACING
                plus, minus = source[j, HALF + i], source[j, HALF - 1 - i]
                even, odd = plus + minus, plus - minus
                t = [even * QUAD_WEIGHT, odd * (QUAD_WEIGHT * xi),
                     even * (QUAD_WEIGHT * xi**2), odd * (QUAD_WEIGHT * xi**3)]
                if i == 0:
                    a0, a1, a2, a3 = t
                else:
                    a0, a1, a2, a3 = a0 + t[0], a1 + t[1], a2 + t[2], a3 + t[3]
            return add_row(sums, a0, a1, a2, a3, speed_of(y), speed_of(z))

        zero = jnp.zeros(f0.shape[2:], jnp.float32)
        sums = (zero,) * MOMENTS
        for c in range(chunks):
            if ready:
                ready[c].wait()
            sums = lax.fori_loop(c * size, (c + 1) * size, one, sums, unroll=math.gcd(2, size))
        return sums

    m1 = moments_of(f0, f_loads)
    for k in range(MOMENTS):
        send1[k] = m1[k]
    loads[0].wait()
    loads[1].wait()
    pl.semaphore_wait(barrier, n_slab * n_vel - 1)

    def scatter(source, first):
        def one(i, _):
            k = lax.rem(rank + i, MOMENTS)
            target = lax.rem(first + k, n_vel)

            @pl.when(target != rank)
            def _():
                pltpu.make_async_remote_copy(
                    src_ref=source.at[k], dst_ref=gather_in.at[rank],
                    send_sem=rs_send.at[0 if source is send1 else 1], recv_sem=rs_recv,
                    device_id={"vel": target}, device_id_type=MESH,
                ).start()

            return 0

        lax.fori_loop(0, MOMENTS, one, 0, unroll=True)

    scatter(send1, first1)

    for step in range(1, n_slab):
        to_slab = lax.rem(slab + step, n_slab)
        pltpu.make_async_remote_copy(
            src_ref=links_ref, dst_ref=links_all.at[slab], send_sem=link_send.at[0, step],
            recv_sem=link_sem.at[0], device_id={"slab": to_slab}, device_id_type=MESH,
        ).start()
        pltpu.make_async_remote_copy(
            src_ref=solid_ref, dst_ref=solid_all.at[slab], send_sem=link_send.at[1, step],
            recv_sem=link_sem.at[1], device_id={"slab": to_slab}, device_id_type=MESH,
        ).start()

    up_half, low_half = pl.ds(HALF, HALF), pl.ds(0, HALF)

    def halo_copy(source, halo, which, half, c):
        part = up_half if half else low_half
        to_slab = slab + 1 if half else slab - 1
        return pltpu.make_async_remote_copy(
            src_ref=source.at[pieces[c], part], dst_ref=halo.at[pieces[c], part],
            send_sem=halo_send.at[which, half, c], recv_sem=halo_recv.at[which, half, c],
            device_id={"slab": to_slab}, device_id_type=MESH,
        )

    def send_halo(source, halo, which, half, c):
        @pl.when(has_above if half else has_below)
        def _():
            halo_copy(source, halo, which, half, c).start()

    def wait_halo(source, halo, which, half, c):
        @pl.when(has_below if half else has_above)
        def _():
            halo_copy(source, halo, which, half, c).wait_recv()

    def wait_halo_send(source, halo, which):
        for half in range(2):
            @pl.when(has_above if half else has_below)
            def _():
                for c in range(chunks):
                    halo_copy(source, halo, which, half, c).wait_send()

    for c in range(chunks):
        send_halo(f0, halo0, 0, 1, c)
        send_halo(f0, halo0, 0, 0, c)

    if n_slab > 1:
        others = pl.ds(0, n_slab - 1)
        pltpu.make_async_copy(links_all.at[others], links_all.at[others], link_sem.at[0]).wait()
        pltpu.make_async_copy(solid_all.at[others], solid_all.at[others], link_sem.at[1]).wait()

    shape = (n_slab,) + f0.shape[2:]
    up = [links_all[:, a].astype(jnp.float32) for a in range(3)]
    at_y = lax.broadcasted_iota(jnp.int32, shape, 1)
    at_z = lax.broadcasted_iota(jnp.int32, shape, 2)
    at_x = lax.broadcasted_iota(jnp.int32, shape, 0)
    low = [
        lower(up[0]),
        jnp.where(at_y == 0, 0.0, rolled(up[1], 1, 1)),
        jnp.where(at_z == 0, 0.0, rolled(up[2], 1, 2)),
    ]
    up_in = [
        jnp.where(at_x == shape[0] - 1, 0.0, up[0]),
        jnp.where(at_y == shape[1] - 1, 0.0, up[1]),
        jnp.where(at_z == shape[2] - 1, 0.0, up[2]),
    ]
    count = up[0] + up[1] + up[2] + low[0] + low[1] + low[2]
    for a in range(3):
        faces[a] = up_in[a]
        faces[3 + a] = low[a]
    faces[6] = 1.0 / (1.0 + COUPLING * count)
    solid = solid_all[...]
    fluid = jnp.where(solid == 0, COURANT, 0.0)
    for a in range(3):
        pred[0] = fluid * low[a]
        pred[1] = fluid * up_in[a]
        pred[2] = fluid * up[a]
        coef[0, a, 0] = pred[0, slab]
        coef[0, a, 1] = pred[1, slab]
        coef[1, a, 0] = pred[2, slab]
        coef[1, a, 1] = pred[0, slab]

    def streamed(source, halo, half, first_row, row_end, finish):
        cells = f0.shape[2:]
        abs_of = [jnp.abs(speed_of(half * HALF + i)) for i in range(HALF)]

        def one(j, carry):
            y, z = row_speeds(j)
            xi_y, xi_z = speed_of(y), speed_of(z)
            sign_y = jnp.where(y >= HALF, 1, 0)
            sign_z = jnp.where(z >= HALF, 1, 0)
            turn_y = jnp.where(y >= HALF, 1, cells[0] - 1)
            turn_z = jnp.where(z >= HALF, 1, cells[1] - 1)
            abs_y, abs_z = jnp.abs(xi_y), jnp.abs(xi_z)
            stay = 1.0 - (abs_y * coef[sign_y, 1, 0] + abs_z * coef[sign_z, 2, 0])
            in_y = abs_y * coef[sign_y, 1, 1]
            in_z = abs_z * coef[sign_z, 2, 1]
            out_x, in_x = coef[half, 0, 0], coef[half, 0, 1]
            extra = finish.row(j, xi_y, xi_z) if finish else None
            for i in range(HALF):
                ix = half * HALF + i
                abs_x = abs_of[i]
                f = source[j, ix]
                value = (
                    f * (stay - abs_x * out_x)
                    + in_y * rolled(f, turn_y, 0)
                    + in_z * rolled(f, turn_z, 1)
                    + abs_x * (in_x * halo[j, ix])
                )
                if finish:
                    finish.store(j, ix, value, extra)
                else:
                    base[j, ix] = value
            return carry

        lax.fori_loop(first_row, row_end, one, 0, unroll=math.gcd(4, row_end - first_row))

    class Goal:
        def __init__(self, target, u, per_temp, s, inv, amp):
            self.target, self.u, self.per_temp, self.s, self.inv, self.amp = target, u, per_temp, s, inv, amp

            def one(i, _):
                c = speed_of(i) - u[0]
                part = c * c * per_temp
                gx[0, i] = jnp.exp(-0.5 * part)
                gx[1, i] = s[0] * c
                gx[2, i] = part
                return 0

            lax.fori_loop(0, NQ, one, 0, unroll=4)

        def row(self, j, xi_y, xi_z):
            c_y, c_z = xi_y - self.u[1], xi_z - self.u[2]
            part = (c_y * c_y + c_z * c_z) * self.per_temp
            return jnp.exp(-0.5 * part) * self.amp, self.s[1] * c_y + self.s[2] * c_z, part - 5.0

        def store(self, j, ix, value, extra):
            height, along, part = extra
            bell = gx[0, ix] * height
            self.target[j, ix] = value * self.inv + bell * (1.0 + (gx[1, ix] + along) * (gx[2, ix] + part))

    lead = jnp.where(has_above, 1, 0)

    def both_halves(body):
        for turn in range(2):
            body(lead if turn == 0 else 1 - lead, turn)

    def wait_dynamic(source, halo, which, half, c):
        @pl.when(half == 1)
        def _():
            wait_halo(source, halo, which, 1, c)

        @pl.when(half == 0)
        def _():
            wait_halo(source, halo, which, 0, c)

    def reduce_and_send(plane, source, everything, which):
        pltpu.make_async_copy(
            gather_in.at[pl.ds(0, n_vel - 1)], gather_in.at[pl.ds(0, n_vel - 1)], rs_recv
        ).wait()
        gather_in[rank] = source[plane]
        total = gather_in[0]
        for v in range(1, n_vel):
            total = total + gather_in[v]
        mine = plane * n_slab + slab
        everything[mine] = total
        for step in range(n_slab):
            to_slab = lax.rem(slab + step, n_slab)

            def one(i, _, to_slab=to_slab, step=step):
                pltpu.make_async_remote_copy(
                    src_ref=everything.at[mine], dst_ref=everything.at[mine],
                    send_sem=ag_send.at[step], recv_sem=ag_recv.at[which],
                    device_id={"slab": to_slab, "vel": lax.rem(rank + i, n_vel)}, device_id_type=MESH,
                ).start()
                return 0

            lax.fori_loop(1 if step == 0 else 0, n_vel, one, 0, unroll=5 if step == 0 else 4)

    def wait_gathered(everything, which, reduces):
        planes = MOMENTS * n_slab

        @pl.when(reduces)
        def _():
            part = everything.at[pl.ds(0, planes - 1)]
            pltpu.make_async_copy(part, part, ag_recv.at[which]).wait()

        @pl.when(jnp.logical_not(reduces))
        def _():
            pltpu.make_async_copy(everything, everything, ag_recv.at[which]).wait()

    def first_pass(half, turn):
        for c in range(chunks):
            wait_dynamic(f0, halo0, 0, half, c)
            streamed(f0, halo0, half, c * size, (c + 1) * size, None)

    first_pass(lead, 0)

    first_pass(1 - lead, 1)
    m2 = moments_of(base)
    for k in range(MOMENTS):
        send2[k] = m2[k]
    scatter(send2, first2)

    @pl.when(reduces1)
    def _():
        reduce_and_send(plane1, send1, all1, 0)

    def predict(moments):
        now = moments
        for _ in range(SWEEPS):
            beside = (
                upper(now) * faces[0] + lower(now) * faces[3]
                + rolled(now, -1, 1) * faces[1] + rolled(now, 1, 1) * faces[4]
                + rolled(now, -1, 2) * faces[2] + rolled(now, 1, 2) * faces[5]
            )
            now = (moments + COUPLING * beside) * faces[6]
        return now

    @pl.when(reduces2)
    def _():
        reduce_and_send(plane2, send2, all2, 1)

    wait_gathered(all1, 0, reduces1)
    state1 = [predict(all1[k * n_slab:(k + 1) * n_slab]) for k in range(MOMENTS)]
    u, per_temp, s, inv, amp = masked_state(state1, solid)

    def own(planes):
        for k, plane in enumerate(planes):
            pred[k] = plane
        return [pred[k, slab] for k in range(len(planes))]

    near = own([*u, per_temp, *s, inv])
    near_amp = own([amp])[0]
    goal = Goal(base, near[0:3], near[3], near[4:7], near[7], near_amp)

    def relax_rows(half):
        def one(j, carry):
            y, z = row_speeds(j)
            extra = goal.row(j, speed_of(y), speed_of(z))
            for i in range(HALF):
                goal.store(j, half * HALF + i, base[j, half * HALF + i], extra)
            return carry

        for c in range(chunks):
            lax.fori_loop(c * size, (c + 1) * size, one, 0, unroll=math.gcd(4, size))
            for side in range(2):
                @pl.when(half == side)
                def _(side=side):
                    send_halo(base, halo1, 1, side, c)

    relax_rows(lead)

    relax_rows(1 - lead)

    target = goal_moments(u, per_temp, s, amp)

    wait_gathered(all2, 1, reduces2)
    state2 = [
        predict(all2[k * n_slab:(k + 1) * n_slab] * inv + target[k]) for k in range(MOMENTS)
    ]
    u, per_temp, s, inv, amp = masked_state(state2, solid)
    near = own([*u, per_temp, *s, inv])
    near_amp = own([amp])[0]
    final = Goal(out_ref, near[0:3], near[3], near[4:7], near[7], near_amp)

    def last_pass(half, turn):
        for c in range(chunks):
            wait_dynamic(base, halo1, 1, half, c)
            streamed(base, halo1, half, c * size, (c + 1) * size, final)

    both_halves(last_pass)

    wait_halo_send(f0, halo0, 0)
    wait_halo_send(base, halo1, 1)
    for step in range(1, n_slab):
        pltpu.make_async_copy(links_all.at[0], links_all.at[0], link_send.at[0, step]).wait()
        pltpu.make_async_copy(solid_all.at[0], solid_all.at[0], link_send.at[1, step]).wait()
    for which, reduces in ((0, reduces1), (1, reduces2)):
        source = send1 if which == 0 else send2

        @pl.when(reduces)
        def _():
            part = source.at[pl.ds(0, MOMENTS - 1)]
            pltpu.make_async_copy(part, part, rs_send.at[which]).wait()
            for step in range(n_slab):
                part = gather_in.at[pl.ds(0, n_vel - 1 if step == 0 else n_vel)]
                pltpu.make_async_copy(part, part, ag_send.at[step]).wait()

        @pl.when(jnp.logical_not(reduces))
        def _():
            pltpu.make_async_copy(source, source, rs_send.at[which]).wait()


def body(f_start, links, solid):
    n_slab, n_vel = lax.axis_size("slab"), lax.axis_size("vel")
    vel_local, planes = f_start.shape[:2]
    cells = f_start.shape[2:]
    rows = vel_local // NQ
    assert planes == 1 and rows * NQ == vel_local and rows % 2 == 0 and n_vel >= 2 * MOMENTS
    f32, vmem, dma = jnp.float32, pltpu.VMEM, pltpu.SemaphoreType.DMA
    chunks = math.gcd(4, rows)
    block = (rows, NQ) + cells
    grid = (n_slab,) + cells
    any_spec = pl.BlockSpec(memory_space=pltpu.HBM)
    out = pl.pallas_call(
        functools.partial(kernel, n_slab, n_vel),
        out_shape=jax.ShapeDtypeStruct(block, f32),
        in_specs=[any_spec] * 3,
        out_specs=pl.BlockSpec(memory_space=pltpu.VMEM),
        scratch_shapes=[
            vmem(block, f32), vmem(block, f32), vmem(block, f32), vmem(block, f32),
            vmem((n_slab, 3) + cells, jnp.int32), vmem(grid, jnp.int32),
            vmem((MOMENTS,) + cells, f32), vmem((MOMENTS,) + cells, f32),
            vmem((n_vel,) + cells, f32),
            vmem((MOMENTS * n_slab,) + cells, f32), vmem((MOMENTS * n_slab,) + cells, f32),
            vmem((7,) + grid, f32), vmem((2, 3, 2) + cells, f32), vmem((3, NQ) + cells, f32),
            vmem((MOMENTS,) + grid, f32),
            dma((chunks,)), dma((2,)), dma((2,)), dma((2, n_slab)), dma((2, 2, chunks)), dma((2, 2, chunks)), dma, dma((2,)),
            dma((2,)), dma((n_slab,)),
        ],
        compiler_params=pltpu.CompilerParams(
            collective_id=0, has_side_effects=True, vmem_limit_bytes=32 * 1024 * 1024
        ),
    )(*(
        pltpu.with_memory_space_constraint(x, pltpu.HBM)
        for x in (f_start.reshape(block), links.reshape((3,) + cells), solid.reshape(cells))
    ))
    return out.reshape(f_start.shape)


def solution(mesh):
    in_specs = (P("vel", "slab", None, None), P(None, "slab", None, None), P("slab", None, None))
    out_specs = P("vel", "slab", None, None)
    return jax.shard_map(body, mesh=mesh, in_specs=in_specs, out_specs=out_specs, check_vma=False)
```

```python
import functools
import math

import jax
import jax.numpy as jnp
from jax import lax
from jax.experimental import pallas as pl
from jax.experimental.pallas import tpu as pltpu
from jax.sharding import PartitionSpec as P

NQ = 16
HALF = NQ // 2
SWEEPS = 2
MOMENTS = 8

SPACING = 0.6
COUPLING = 1.0
COURANT = 0.06
RELAXATION_FREQ = 0.5
VISCOUS_TO_HEAT = 2.0 / 3.0
QUAD_WEIGHT = SPACING**3 / (2.0 * math.pi) ** 1.5

MESH = pl.DeviceIdType.MESH


def speed_of(index):
    return (index.astype(jnp.float32) - (NQ - 1) / 2.0) * SPACING


def rolled(cells, shift, axis):
    size = cells.shape[axis]
    return pltpu.roll(cells, shift % size if isinstance(shift, int) else shift, axis)


def upper(cells):
    return jnp.concatenate([cells[1:], jnp.zeros_like(cells[:1])], axis=0)


def lower(cells):
    return jnp.concatenate([jnp.zeros_like(cells[:1]), cells[:-1]], axis=0)


def macro_state(predicted):
    rho = predicted[0]
    per_rho = 1.0 / rho
    u = [predicted[1 + a] * per_rho for a in range(3)]
    energy = predicted[4]
    temp = (2.0 * energy * per_rho - (u[0] * u[0] + u[1] * u[1] + u[2] * u[2])) / 3.0
    pressure = rho * temp
    nu = RELAXATION_FREQ * rho * jnp.exp(0.28 * jnp.log(temp))
    scale = (1.0 - VISCOUS_TO_HEAT) / (5.0 * pressure * temp)
    s = [(predicted[5 + a] - u[a] * (energy + pressure)) * scale for a in range(3)]
    root = lax.rsqrt(temp)
    return u, temp, nu, s, rho * (root * root * root)


def masked_state(predicted, solid):
    u, temp, nu, s, height = macro_state(predicted)
    fluid = solid == 0
    per_temp = jnp.where(fluid, 1.0 / temp, 1.0)
    u = [jnp.where(fluid, x, 0.0) for x in u]
    s = [jnp.where(fluid, x, 0.0) for x in s]
    inv = jnp.where(fluid, 1.0 / (1.0 + nu), 1.0)
    amp = jnp.where(fluid, height * (nu / (1.0 + nu)), 0.0)
    return u, per_temp, s, inv, amp


def goal_moments(u, per_temp, s, amp):
    def one(i, sums):
        xi = speed_of(i)
        new = []
        for a in range(3):
            c = xi - u[a]
            term = jnp.exp(-0.5 * (c * c * per_temp))
            row = [sums[a][0] + term]
            for k in range(1, 7):
                term = term * c
                row.append(sums[a][k] + term)
            new.append(tuple(row))
        return tuple(new)

    zero = jnp.zeros_like(per_temp)
    line = lax.fori_loop(0, NQ, one, tuple((zero,) * 7 for _ in range(3)), unroll=4)
    pairs, products, heats, lifts = {}, {}, {}, {}

    def add(m, a, n=1):
        return tuple(k + n * (a == d) for d, k in enumerate(m))

    def f(m):
        if m not in products:
            if m[:2] not in pairs:
                pairs[m[:2]] = line[0][m[0]] * line[1][m[1]]
            products[m] = pairs[m[:2]] * line[2][m[2]]
        return products[m]

    def q(m):
        if m not in heats:
            heats[m] = f(add(m, 0, 2)) + f(add(m, 1, 2)) + f(add(m, 2, 2))
        return heats[m]

    def lift(m):
        if m not in lifts:
            lifts[m] = per_temp * q(m) - 5.0 * f(m)
        return lifts[m]

    def total(m):
        out = f(m)
        for a in range(3):
            out = out + s[a] * lift(add(m, a))
        return out

    def total_q(m):
        out = q(m)
        for a in range(3):
            up = add(m, a)
            out = out + s[a] * (lift(add(up, 0, 2)) + lift(add(up, 1, 2)) + lift(add(up, 2, 2)))
        return out

    origin = (0, 0, 0)
    weight = amp * QUAD_WEIGHT
    p0 = total(origin) * weight
    p1 = [total(add(origin, a)) * weight for a in range(3)]
    p2 = {}
    for a in range(3):
        for b in range(a, 3):
            p2[a, b] = p2[b, a] = total(add(add(origin, a), b)) * weight
    p3 = [total_q(add(origin, a)) * weight for a in range(3)]
    half_uu = 0.5 * (u[0] * u[0] + u[1] * u[1] + u[2] * u[2])
    energy = (
        0.5 * (p2[0, 0] + p2[1, 1] + p2[2, 2])
        + (u[0] * p1[0] + u[1] * p1[1] + u[2] * p1[2])
        + half_uu * p0
    )
    out = [p0] + [p1[a] + u[a] * p0 for a in range(3)] + [energy]
    for a in range(3):
        out.append(
            0.5 * p3[a]
            + (u[0] * p2[a, 0] + u[1] * p2[a, 1] + u[2] * p2[a, 2])
            + half_uu * p1[a]
            + u[a] * energy
        )
    return out


def kernel(
    n_slab, n_vel, f_ref, links_ref, solid_ref, out_ref,
    f0, base, halo0, halo1, links_all, solid_all, send1, send2, gather_in, all1, all2,
    faces, coef, gx, pred,
    load_sem, link_sem, link_send, halo_recv, halo_send, rs_recv, rs_send, ag_recv, ag_send, fwd_recv, fwd_send,
):
    slab = lax.axis_index("slab")
    rank = lax.axis_index("vel")
    rows = f_ref.shape[0]
    first1 = n_vel // 2 - MOMENTS // 2
    first2 = n_vel // 2 + MOMENTS // 2
    plane1 = rank - first1
    plane2 = lax.rem(rank - first2 + n_vel, n_vel)
    reduces1 = (plane1 >= 0) & (plane1 < MOMENTS)
    reduces2 = plane2 < MOMENTS
    has_below = slab > 0
    has_above = slab < n_slab - 1

    def start_all(copies):
        for copy in copies:
            copy.start()

    loads = [
        pltpu.make_async_copy(f_ref, f0, load_sem.at[0]),
        pltpu.make_async_copy(links_ref, links_all.at[slab], load_sem.at[1]),
        pltpu.make_async_copy(solid_ref, solid_all.at[slab], load_sem.at[2]),
    ]
    start_all(loads)

    barrier = pltpu.get_barrier_semaphore()
    for step in range(n_slab):
        to_slab = lax.rem(slab + step, n_slab)

        def greet(i, _, to_slab=to_slab):
            pl.semaphore_signal(
                barrier, inc=1, device_id={"slab": to_slab, "vel": lax.rem(rank + i, n_vel)},
                device_id_type=MESH,
            )
            return 0

        lax.fori_loop(1 if step == 0 else 0, n_vel, greet, 0, unroll=5 if step == 0 else 4)

    def clear(low):
        def one(j, _):
            for i in range(HALF):
                zero = jnp.zeros(f0.shape[2:], jnp.float32)
                halo0[j, low + i] = zero
                halo1[j, low + i] = zero
            return 0

        lax.fori_loop(0, rows, one, 0)

    @pl.when(jnp.logical_not(has_below))
    def _():
        clear(HALF)

    @pl.when(jnp.logical_not(has_above))
    def _():
        clear(0)

    def row_speeds(j):
        row = rank * rows + j
        return lax.rem(row, NQ), lax.div(row, NQ)

    def add_row(sums, a0, a1, a2, a3, xi_y, xi_z):
        r = xi_y * xi_y + xi_z * xi_z
        e = 0.5 * (a2 + r * a0)
        return (
            sums[0] + a0, sums[1] + a1, sums[2] + xi_y * a0, sums[3] + xi_z * a0,
            sums[4] + e, sums[5] + 0.5 * (a3 + r * a1), sums[6] + xi_y * e, sums[7] + xi_z * e,
        )

    def moments_of(source):
        def one(j, sums):
            y, z = row_speeds(j)
            a0 = a1 = a2 = a3 = None
            for i in range(HALF):
                xi = (i + 0.5) * SPACING
                plus, minus = source[j, HALF + i], source[j, HALF - 1 - i]
                even, odd = plus + minus, plus - minus
                t = [even * QUAD_WEIGHT, odd * (QUAD_WEIGHT * xi),
                     even * (QUAD_WEIGHT * xi**2), odd * (QUAD_WEIGHT * xi**3)]
                if i == 0:
                    a0, a1, a2, a3 = t
                else:
                    a0, a1, a2, a3 = a0 + t[0], a1 + t[1], a2 + t[2], a3 + t[3]
            return add_row(sums, a0, a1, a2, a3, speed_of(y), speed_of(z))

        zero = jnp.zeros(f0.shape[2:], jnp.float32)
        return lax.fori_loop(0, rows, one, (zero,) * MOMENTS, unroll=2)

    loads[0].wait()
    m1 = moments_of(f0)
    for k in range(MOMENTS):
        send1[k] = m1[k]
    loads[1].wait()
    loads[2].wait()
    pl.semaphore_wait(barrier, n_slab * n_vel - 1)

    def scatter(source, first):
        def one(i, _):
            k = lax.rem(rank + i, MOMENTS)
            target = lax.rem(first + k, n_vel)

            @pl.when(target != rank)
            def _():
                pltpu.make_async_remote_copy(
                    src_ref=source.at[k], dst_ref=gather_in.at[rank],
                    send_sem=rs_send.at[0 if source is send1 else 1], recv_sem=rs_recv,
                    device_id={"vel": target}, device_id_type=MESH,
                ).start()

            return 0

        lax.fori_loop(0, MOMENTS, one, 0, unroll=True)

    scatter(send1, first1)

    for step in range(1, n_slab):
        to_slab = lax.rem(slab + step, n_slab)
        pltpu.make_async_remote_copy(
            src_ref=links_ref, dst_ref=links_all.at[slab], send_sem=link_send.at[0, step],
            recv_sem=link_sem.at[0], device_id={"slab": to_slab}, device_id_type=MESH,
        ).start()
        pltpu.make_async_remote_copy(
            src_ref=solid_ref, dst_ref=solid_all.at[slab], send_sem=link_send.at[1, step],
            recv_sem=link_sem.at[1], device_id={"slab": to_slab}, device_id_type=MESH,
        ).start()

    up_half, low_half = pl.ds(HALF, HALF), pl.ds(0, HALF)

    def halo_copy(source, halo, which, half):
        part = up_half if half else low_half
        to_slab = slab + 1 if half else slab - 1
        return pltpu.make_async_remote_copy(
            src_ref=source.at[:, part], dst_ref=halo.at[:, part],
            send_sem=halo_send.at[which, half], recv_sem=halo_recv.at[which, half],
            device_id={"slab": to_slab}, device_id_type=MESH,
        )

    def send_halo(source, halo, which):
        @pl.when(has_above)
        def _():
            halo_copy(source, halo, which, 1).start()

        @pl.when(has_below)
        def _():
            halo_copy(source, halo, which, 0).start()

    def wait_halo(source, halo, which, half):
        @pl.when(has_below if half else has_above)
        def _():
            halo_copy(source, halo, which, half).wait_recv()

    def wait_halo_send(source, halo, which):
        @pl.when(has_above)
        def _():
            halo_copy(source, halo, which, 1).wait_send()

        @pl.when(has_below)
        def _():
            halo_copy(source, halo, which, 0).wait_send()

    send_halo(f0, halo0, 0)

    if n_slab > 1:
        others = pl.ds(0, n_slab - 1)
        pltpu.make_async_copy(links_all.at[others], links_all.at[others], link_sem.at[0]).wait()
        pltpu.make_async_copy(solid_all.at[others], solid_all.at[others], link_sem.at[1]).wait()

    shape = (n_slab,) + f0.shape[2:]
    up = [links_all[:, a].astype(jnp.float32) for a in range(3)]
    at_y = lax.broadcasted_iota(jnp.int32, shape, 1)
    at_z = lax.broadcasted_iota(jnp.int32, shape, 2)
    at_x = lax.broadcasted_iota(jnp.int32, shape, 0)
    low = [
        lower(up[0]),
        jnp.where(at_y == 0, 0.0, rolled(up[1], 1, 1)),
        jnp.where(at_z == 0, 0.0, rolled(up[2], 1, 2)),
    ]
    up_in = [
        jnp.where(at_x == shape[0] - 1, 0.0, up[0]),
        jnp.where(at_y == shape[1] - 1, 0.0, up[1]),
        jnp.where(at_z == shape[2] - 1, 0.0, up[2]),
    ]
    count = up[0] + up[1] + up[2] + low[0] + low[1] + low[2]
    for a in range(3):
        faces[a] = up_in[a]
        faces[3 + a] = low[a]
    faces[6] = 1.0 / (1.0 + COUPLING * count)
    solid = solid_all[...]
    fluid = jnp.where(solid == 0, COURANT, 0.0)
    for a in range(3):
        pred[0] = fluid * low[a]
        pred[1] = fluid * up_in[a]
        pred[2] = fluid * up[a]
        coef[0, a, 0] = pred[0, slab]
        coef[0, a, 1] = pred[1, slab]
        coef[1, a, 0] = pred[2, slab]
        coef[1, a, 1] = pred[0, slab]

    def streamed(source, halo, half, first_row, row_end, finish):
        cells = f0.shape[2:]
        abs_of = [jnp.abs(speed_of(half * HALF + i)) for i in range(HALF)]

        def one(j, carry):
            y, z = row_speeds(j)
            xi_y, xi_z = speed_of(y), speed_of(z)
            sign_y = jnp.where(y >= HALF, 1, 0)
            sign_z = jnp.where(z >= HALF, 1, 0)
            turn_y = jnp.where(y >= HALF, 1, cells[0] - 1)
            turn_z = jnp.where(z >= HALF, 1, cells[1] - 1)
            abs_y, abs_z = jnp.abs(xi_y), jnp.abs(xi_z)
            stay = 1.0 - (abs_y * coef[sign_y, 1, 0] + abs_z * coef[sign_z, 2, 0])
            in_y = abs_y * coef[sign_y, 1, 1]
            in_z = abs_z * coef[sign_z, 2, 1]
            out_x, in_x = coef[half, 0, 0], coef[half, 0, 1]
            extra = finish.row(j, xi_y, xi_z) if finish else None
            for i in range(HALF):
                ix = half * HALF + i
                abs_x = abs_of[i]
                f = source[j, ix]
                value = (
                    f * (stay - abs_x * out_x)
                    + in_y * rolled(f, turn_y, 0)
                    + in_z * rolled(f, turn_z, 1)
                    + abs_x * (in_x * halo[j, ix])
                )
                if finish:
                    finish.store(j, ix, value, extra)
                else:
                    base[j, ix] = value
            return carry

        lax.fori_loop(first_row, row_end, one, 0, unroll=math.gcd(4, row_end - first_row))

    class Goal:
        def __init__(self, target, u, per_temp, s, inv, amp):
            self.target, self.u, self.per_temp, self.s, self.inv, self.amp = target, u, per_temp, s, inv, amp

            def one(i, _):
                c = speed_of(i) - u[0]
                part = c * c * per_temp
                gx[0, i] = jnp.exp(-0.5 * part)
                gx[1, i] = s[0] * c
                gx[2, i] = part
                return 0

            lax.fori_loop(0, NQ, one, 0, unroll=4)

        def row(self, j, xi_y, xi_z):
            c_y, c_z = xi_y - self.u[1], xi_z - self.u[2]
            part = (c_y * c_y + c_z * c_z) * self.per_temp
            return jnp.exp(-0.5 * part) * self.amp, self.s[1] * c_y + self.s[2] * c_z, part - 5.0

        def store(self, j, ix, value, extra):
            height, along, part = extra
            bell = gx[0, ix] * height
            self.target[j, ix] = value * self.inv + bell * (1.0 + (gx[1, ix] + along) * (gx[2, ix] + part))

    lead = jnp.where(has_above, 1, 0)

    def both_halves(body):
        for turn in range(2):
            body(lead if turn == 0 else 1 - lead, turn)

    def wait_dynamic(source, halo, which, half):
        @pl.when(half == 1)
        def _():
            wait_halo(source, halo, which, 1)

        @pl.when(half == 0)
        def _():
            wait_halo(source, halo, which, 0)

    def reduce_and_send(plane, source, everything, which):
        pltpu.make_async_copy(
            gather_in.at[pl.ds(0, n_vel - 1)], gather_in.at[pl.ds(0, n_vel - 1)], rs_recv
        ).wait()
        gather_in[rank] = source[plane]
        total = gather_in[0]
        for v in range(1, n_vel):
            total = total + gather_in[v]
        mine = slab * MOMENTS + plane
        everything[mine] = total
        def one(i, _):
            pltpu.make_async_remote_copy(
                src_ref=everything.at[mine], dst_ref=everything.at[mine],
                send_sem=ag_send.at[0], recv_sem=ag_recv.at[which],
                device_id={"vel": lax.rem(rank + i, n_vel)}, device_id_type=MESH,
            ).start()
            return 0

        lax.fori_loop(1, n_vel, one, 0, unroll=5)

    def wait_gathered(everything, which, reduces):
        @pl.when(reduces)
        def _():
            part = everything.at[pl.ds(0, MOMENTS - 1)]
            pltpu.make_async_copy(part, part, ag_recv.at[which]).wait()

        @pl.when(jnp.logical_not(reduces))
        def _():
            part = everything.at[pl.ds(0, MOMENTS)]
            pltpu.make_async_copy(part, part, ag_recv.at[which]).wait()

        own_sums = everything.at[pl.ds(slab * MOMENTS, MOMENTS)]
        for step in range(1, n_slab):
            pltpu.make_async_remote_copy(
                src_ref=own_sums, dst_ref=own_sums, send_sem=fwd_send.at[which, step],
                recv_sem=fwd_recv.at[which], device_id={"slab": lax.rem(slab + step, n_slab)},
                device_id_type=MESH,
            ).start()
        if n_slab > 1:
            part = everything.at[pl.ds(0, MOMENTS * (n_slab - 1))]
            pltpu.make_async_copy(part, part, fwd_recv.at[which]).wait()

    def over_slabs(everything, k):
        return jnp.stack([everything[p * MOMENTS + k] for p in range(n_slab)])

    def first_pass(half, turn):
        wait_dynamic(f0, halo0, 0, half)
        streamed(f0, halo0, half, 0, rows, None)

    first_pass(lead, 0)

    first_pass(1 - lead, 1)
    m2 = moments_of(base)
    for k in range(MOMENTS):
        send2[k] = m2[k]
    scatter(send2, first2)

    @pl.when(reduces1)
    def _():
        reduce_and_send(plane1, send1, all1, 0)

    def predict(moments):
        now = moments
        for _ in range(SWEEPS):
            beside = (
                upper(now) * faces[0] + lower(now) * faces[3]
                + rolled(now, -1, 1) * faces[1] + rolled(now, 1, 1) * faces[4]
                + rolled(now, -1, 2) * faces[2] + rolled(now, 1, 2) * faces[5]
            )
            now = (moments + COUPLING * beside) * faces[6]
        return now

    @pl.when(reduces2)
    def _():
        reduce_and_send(plane2, send2, all2, 1)

    wait_gathered(all1, 0, reduces1)
    state1 = [predict(over_slabs(all1, k)) for k in range(MOMENTS)]
    u, per_temp, s, inv, amp = masked_state(state1, solid)

    def own(planes):
        for k, plane in enumerate(planes):
            pred[k] = plane
        return [pred[k, slab] for k in range(len(planes))]

    near = own([*u, per_temp, *s, inv])
    near_amp = own([amp])[0]
    goal = Goal(base, near[0:3], near[3], near[4:7], near[7], near_amp)

    def relax_rows(half):
        def one(j, carry):
            y, z = row_speeds(j)
            extra = goal.row(j, speed_of(y), speed_of(z))
            for i in range(HALF):
                goal.store(j, half * HALF + i, base[j, half * HALF + i], extra)
            return carry

        lax.fori_loop(0, rows, one, 0, unroll=math.gcd(4, rows))

    relax_rows(lead)

    @pl.when(lead == 1)
    def _():
        @pl.when(has_above)
        def _():
            halo_copy(base, halo1, 1, 1).start()

    @pl.when(lead == 0)
    def _():
        @pl.when(has_below)
        def _():
            halo_copy(base, halo1, 1, 0).start()

    relax_rows(1 - lead)

    @pl.when(jnp.logical_and(lead == 1, has_below))
    def _():
        halo_copy(base, halo1, 1, 0).start()

    target = goal_moments(u, per_temp, s, amp)

    wait_gathered(all2, 1, reduces2)
    state2 = [
        predict(over_slabs(all2, k) * inv + target[k]) for k in range(MOMENTS)
    ]
    u, per_temp, s, inv, amp = masked_state(state2, solid)
    near = own([*u, per_temp, *s, inv])
    near_amp = own([amp])[0]
    final = Goal(out_ref, near[0:3], near[3], near[4:7], near[7], near_amp)

    def last_pass(half, turn):
        wait_dynamic(base, halo1, 1, half)
        streamed(base, halo1, half, 0, rows, final)

    both_halves(last_pass)

    wait_halo_send(f0, halo0, 0)
    wait_halo_send(base, halo1, 1)
    for step in range(1, n_slab):
        pltpu.make_async_copy(links_all.at[0], links_all.at[0], link_send.at[0, step]).wait()
        pltpu.make_async_copy(solid_all.at[0], solid_all.at[0], link_send.at[1, step]).wait()
    for which, reduces in ((0, reduces1), (1, reduces2)):
        for step in range(1, n_slab):
            pltpu.make_async_copy(send1, send1, fwd_send.at[which, step]).wait()
        source = send1 if which == 0 else send2

        @pl.when(reduces)
        def _():
            part = source.at[pl.ds(0, MOMENTS - 1)]
            pltpu.make_async_copy(part, part, rs_send.at[which]).wait()
            part = gather_in.at[pl.ds(0, n_vel - 1)]
            pltpu.make_async_copy(part, part, ag_send.at[0]).wait()

        @pl.when(jnp.logical_not(reduces))
        def _():
            pltpu.make_async_copy(source, source, rs_send.at[which]).wait()


def body(f_start, links, solid):
    n_slab, n_vel = lax.axis_size("slab"), lax.axis_size("vel")
    vel_local, planes = f_start.shape[:2]
    cells = f_start.shape[2:]
    rows = vel_local // NQ
    assert planes == 1 and rows * NQ == vel_local and rows % 2 == 0 and n_vel >= 2 * MOMENTS
    f32, vmem, dma = jnp.float32, pltpu.VMEM, pltpu.SemaphoreType.DMA
    block = (rows, NQ) + cells
    grid = (n_slab,) + cells
    any_spec = pl.BlockSpec(memory_space=pltpu.HBM)
    out = pl.pallas_call(
        functools.partial(kernel, n_slab, n_vel),
        out_shape=jax.ShapeDtypeStruct(block, f32),
        in_specs=[any_spec] * 3,
        out_specs=pl.BlockSpec(memory_space=pltpu.VMEM),
        scratch_shapes=[
            vmem(block, f32), vmem(block, f32), vmem(block, f32), vmem(block, f32),
            vmem((n_slab, 3) + cells, jnp.int32), vmem(grid, jnp.int32),
            vmem((MOMENTS,) + cells, f32), vmem((MOMENTS,) + cells, f32),
            vmem((n_vel,) + cells, f32),
            vmem((MOMENTS * n_slab,) + cells, f32), vmem((MOMENTS * n_slab,) + cells, f32),
            vmem((7,) + grid, f32), vmem((2, 3, 2) + cells, f32), vmem((3, NQ) + cells, f32),
            vmem((MOMENTS,) + grid, f32),
            dma((3,)), dma((2,)), dma((2, n_slab)), dma((2, 2)), dma((2, 2)), dma, dma((2,)),
            dma((2,)), dma((1,)), dma((2,)), dma((2, n_slab)),
        ],
        compiler_params=pltpu.CompilerParams(
            collective_id=0, has_side_effects=True, vmem_limit_bytes=32 * 1024 * 1024
        ),
    )(*(
        pltpu.with_memory_space_constraint(x, pltpu.HBM)
        for x in (f_start.reshape(block), links.reshape((3,) + cells), solid.reshape(cells))
    ))
    return out.reshape(f_start.shape)


def solution(mesh):
    in_specs = (P("vel", "slab", None, None), P(None, "slab", None, None), P("slab", None, None))
    out_specs = P("vel", "slab", None, None)
    return jax.shard_map(body, mesh=mesh, in_specs=in_specs, out_specs=out_specs, check_vma=False)
```
